32 devices in a mesh: groups: 2 (over y), row: 4 (over z), col: 4 (over x, core).
Axes of the slice: x: 2, y: 2, z: 4, core: 2. Of those that a mesh axis runs over, the one named last changes fastest.
Arguments:
- features: bfloat16 [8, 2048, 256], P(('groups', 'row'), 'col'), parts along dimension 0, may hold values from -6 to 6
- tile_values: bfloat16 [8, 4, 1024, 4096], P(('groups', 'row'), 'col'), parts along dimension 0, may hold values from -0.125 to 0.125
- tile_rows: int32 [8, 4, 1024], P(('groups', 'row'), 'col'), parts along dimension 0, may hold values from 0 to 31
- tile_cols: int32 [8, 4, 1024], P(('groups', 'row'), 'col'), parts along dimension 0, may hold values from 0 to 31
- counts: int32 [8, 4], P(('groups', 'row'), 'col'), parts along dimension 0, may hold values from 128 to 1024, as said below
- weight: bfloat16 [256, 256], replicated, may hold values from -0.375 to 0.375
- bias: float32 [256], replicated, may hold values from -3 to 3
Outputs:
- layer_out: bfloat16 [8, 2048, 256], P(('groups', 'col'), 'row'), parts along dimension 0
The draws below stay inside these ranges and needn't reach their ends.
There are 2 independent parts, one for each index of `groups`. The reference program is written for one: setup_inputs(seed, part) draws one part's arguments, and reference() takes and returns one part's arrays. A program takes and returns all parts, laid end to end along the dimension named above; an argument that names none is the same for every part. Nothing has to cross between parts.
Inputs may be any that keep to these rules, and one draw needn't show every extreme that they name: Slots at or past counts[r, c] hold values that are to be ignored; coordinate pairs may repeat within a cell, and repeated tiles add. In every draw one grid cell has exactly 1024 live slots.
All inputs are finite; a program needn't handle non-finite values.
Results may differ from the reference program's by a relative error of at most 0.0046.
Values may be sent and summed in bfloat16 or wider, within the bound.
A program may use at most 128 MiB of HBM per device.

```python
import jax
import jax.numpy as jnp
from jax import lax

F = 256
TILE = 64
P_SIZE = 512
TILES = 1024
N_ROW = 4
N_COL = 4


def draw_counts(key, part):
    first_key = jax.random.fold_in(key, 11)
    second_key = jax.random.fold_in(key, 23)
    third_key = jax.random.fold_in(key, 37)
    left_draw = jax.random.randint(first_key, (N_ROW * N_COL,), 1, TILES + 1, dtype=jnp.int32)
    right_draw = jax.random.randint(second_key, (N_ROW * N_COL,), 1, TILES + 1, dtype=jnp.int32)
    loads = jnp.maximum(left_draw * right_draw // TILES, TILES // 8)
    chosen = jax.random.randint(third_key, (), 0, N_ROW * N_COL, dtype=jnp.int32)
    loads = loads.at[chosen].set(TILES)
    return loads.reshape(N_ROW, N_COL).astype(jnp.int32)


def touch_ends(array, key, low, top_value):
    longest = array.shape.index(max(array.shape))
    spots = []
    for shift in (0, 1):
        where = [jax.random.randint(jax.random.fold_in(key, axis), (), 0, length) for axis, length in enumerate(array.shape)]
        where[longest] = (where[longest] + shift) % array.shape[longest]
        spots.append(tuple(where))
    return array.at[spots[0]].set(low).at[spots[1]].set(top_value)


def level_of(own_key, extent, split, least, high):
    def one(axis_at, blocks):
        heights = jax.random.uniform(jax.random.fold_in(jax.random.fold_in(own_key, 6), axis_at), (blocks,), jnp.float32, least / len(split), high / len(split))
        return jnp.repeat(jnp.exp(heights), extent[axis_at] // blocks).reshape((-1,) + (1,) * (len(extent) - axis_at - 1))

    gain = one(*split[0])
    for cut in split[1:]:
        gain = gain * one(*cut)
    return gain


def scatter_about(stream_key, shape, width, bound, shards=(), held_as=jnp.bfloat16):
    gain = level_of(stream_key, shape, shards, -0.22, 0.18) if shards else 1.0
    entries = jax.random.normal(stream_key, shape, jnp.float32) * width * gain
    return jnp.minimum(jnp.maximum(entries, -bound), bound).astype(held_as)


def setup_inputs(seed: int = 0, part: int = 0) -> dict:
    key_list = jax.random.split(jax.random.key(seed), 8)
    own_keys = jax.random.split(jax.random.fold_in(key_list[7], part), 8)
    return {
        "features": scatter_about(own_keys[0], (N_ROW, N_COL * P_SIZE, F), 1.0, 6.0, ((0, 4), (1, 4))),
        "tile_values": scatter_about(own_keys[1], (N_ROW, N_COL, TILES, TILE * TILE), (TILES * TILE * TILE // (4 * P_SIZE)) ** -0.5, 0.125, ((0, 4), (1, 4))),
        "tile_rows": touch_ends(jax.random.randint(own_keys[2], (N_ROW, N_COL, TILES), 0, N_ROW * P_SIZE // TILE), jax.random.fold_in(own_keys[2], 1), 0, (N_ROW * P_SIZE // TILE) - 1).astype(jnp.int32),
        "tile_cols": touch_ends(jax.random.randint(own_keys[3], (N_ROW, N_COL, TILES), 0, N_COL * P_SIZE // TILE), jax.random.fold_in(own_keys[3], 1), 0, (N_COL * P_SIZE // TILE) - 1).astype(jnp.int32),
        "counts": draw_counts(jax.random.fold_in(jax.random.fold_in(key_list[7], part), 71), part),
        "weight": scatter_about(key_list[5], (F, F), F ** -0.5, 0.375),
        "bias": scatter_about(key_list[6], (F,), 0.5, 3.0, (), jnp.float32),
    }


def reference(features, tile_values, tile_rows, tile_cols, counts, weight, bias):
    block_size = min(128, TILES)
    out_tiles = N_ROW * P_SIZE // TILE
    running = jnp.zeros((N_COL, out_tiles, TILE, F), jnp.float32)
    cells = N_ROW * N_COL
    all_values = tile_values.reshape(cells, TILES, TILE * TILE)
    all_rows = tile_rows.reshape(cells, TILES).astype(jnp.int32)
    all_cols = tile_cols.reshape(cells, TILES).astype(jnp.int32)
    all_counts = counts.reshape(cells).astype(jnp.int32)
    cell_index = jnp.arange(cells, dtype=jnp.int32)
    grid_rows = cell_index // N_COL
    grid_cols = cell_index % N_COL

    def cell_step(running, item):
        values, tile_row, tile_col, live_count, grid_row, grid_col = item
        source = lax.dynamic_index_in_dim(features, grid_row, 0, keepdims=False).reshape(N_COL * P_SIZE // TILE, TILE, F)

        def block_step(block_index, running):
            first_slot = (block_index * block_size).astype(jnp.int32)
            tile_block = lax.dynamic_slice_in_dim(values, first_slot, block_size, 0).reshape(block_size, TILE, TILE).astype(jnp.float32)
            target_rows = lax.dynamic_slice_in_dim(tile_row, first_slot, block_size, 0)
            source_cols = lax.dynamic_slice_in_dim(tile_col, first_slot, block_size, 0)
            inputs = source[source_cols].astype(jnp.float32)
            products = jnp.einsum('bij,bjf->bif', tile_block, inputs, precision=lax.Precision.HIGHEST)
            is_live = first_slot + jnp.arange(block_size, dtype=jnp.int32) < live_count
            target = jnp.where(is_live, target_rows, out_tiles)
            return running.at[grid_col, target].add(products, mode="drop")

        block_count = (live_count + block_size - 1) // block_size
        running = lax.fori_loop(0, block_count, block_step, running)
        return running, None

    running, unused = lax.scan(cell_step, running, (all_values, all_rows, all_cols, all_counts, grid_rows, grid_cols))
    hidden = running.reshape(N_COL * N_ROW * P_SIZE, F).astype(jnp.bfloat16)
    mixed = jnp.dot(hidden, weight, preferred_element_type=jnp.float32) + bias.astype(jnp.float32)
    return jnp.maximum(mixed, 0.0).astype(jnp.bfloat16).reshape(N_COL, N_ROW * P_SIZE, F)
```

```python
import functools

import jax
import jax.numpy as jnp
from jax import lax
from jax.experimental import pallas as pl
from jax.experimental.pallas import tpu as pltpu
from jax.sharding import PartitionSpec as P

TILE = 64
LANES = 128
FINAL = 16
LAG = 2
PLAN = (
    "d00", "d01", "d10", "r00", "d11", "s00", "m00", "x00", "m10", "r10", "x10", "l00",
    "l10", "d20", "d21", "m20", "x20", "f00", "s10", "m01", "x01", "f10", "m11", "x11",
    "m21", "x21", "d30", "f20", "d31", "f01", "m30", "x30", "m31", "x31", "f11", "f21",
    "f30", "f31", "l20", "l01", "l11", "l21", "l30", "l31",
)
MESH = pl.DeviceIdType.MESH


def layer_kernel(
    n_row, n_col, piece, counts_hbm, vals_hbm, rows_hbm, cols_hbm, feat_hbm, weight_hbm, bias_hbm,
    out_ref, vals, live, rows_in, cols_in, weight, bias, pick, dense, src, wide, acc, up_in, down_in,
    final, vals_sem, small_sem, own_sem, far_send, far_recv, near_send, near_recv, send_sem, up_sem,
    down_sem,
):
    steps, slots, lanes = vals.shape
    halves, source_rows, part = src.shape
    cuts = far_send.shape[2]
    tiles_in = pick.shape[0]
    piece_rows = feat_hbm.shape[1]
    col_tiles = source_rows // TILE
    row_tiles = tiles_in // col_tiles
    chunk = min(tiles_in, 1024)
    chunk_cols = chunk // row_tiles
    own = row_tiles // n_row
    blocks = lanes // LANES
    units = steps * halves
    chips = n_col // 2
    z = lax.axis_index("row")
    me = lax.axis_index("col")
    core = lax.rem(me, 2)
    sibling = me + 1 - 2 * core

    barrier = pltpu.get_barrier_semaphore()
    for d in range(1, chips):
        pl.semaphore_signal(
            barrier, inc=1, device_id={"col": lax.rem(me + 2 * d, n_col)}, device_id_type=MESH
        )
    pl.semaphore_signal(barrier, inc=1, device_id={"col": sibling}, device_id_type=MESH)

    direct = n_row == 4
    reach = 2 if direct else 1
    for d in range(1, reach + 1):

        @pl.when(z >= d)
        def _():
            pl.semaphore_signal(barrier, inc=1, device_id={"row": z - d}, device_id_type=MESH)

        @pl.when(z < n_row - d)
        def _():
            pl.semaphore_signal(barrier, inc=1, device_id={"row": z + d}, device_id_type=MESH)

    smalls = [
        pltpu.make_async_copy(rows_hbm.at[0], rows_in, small_sem.at[0]),
        pltpu.make_async_copy(cols_hbm.at[0], cols_in, small_sem.at[1]),
        pltpu.make_async_copy(counts_hbm, live, small_sem.at[2]),
        pltpu.make_async_copy(weight_hbm, weight, small_sem.at[3]),
        pltpu.make_async_copy(bias_hbm, bias, small_sem.at[4]),
    ]
    cut_rows = piece_rows // cuts

    def rows_of(index, q, cut):
        first = pl.multiple_of(index * piece_rows + cut * cut_rows, cut_rows)
        return src.at[q, pl.ds(first, cut_rows)]

    def far(d, q, cut):
        return pltpu.make_async_remote_copy(
            src_ref=rows_of(me, q, cut), dst_ref=rows_of(me, q, cut),
            send_sem=far_send.at[d, q, cut], recv_sem=far_recv.at[d, q, cut],
            device_id={"col": lax.rem(me + 2 * d, n_col)}, device_id_type=MESH,
        )

    def near(d, q, cut):
        origin = lax.rem(me + n_col - 2 * d, n_col)
        return pltpu.make_async_remote_copy(
            src_ref=rows_of(origin, q, cut), dst_ref=rows_of(origin, q, cut),
            send_sem=near_send.at[d, q, cut], recv_sem=near_recv.at[d, q, cut],
            device_id={"col": sibling}, device_id_type=MESH,
        )

    def keep(q):
        return pltpu.make_async_copy(
            feat_hbm.at[0, :, pl.ds(q * part, part)],
            src.at[q, pl.ds(pl.multiple_of(me * piece_rows, piece_rows), piece_rows)],
            own_sem.at[q],
        )

    for q in range(halves):
        keep(q).start()
    for copy in smalls[:3]:
        copy.start()

    def load(step):
        return pltpu.make_async_copy(
            vals_hbm.at[0, 0, :, pl.ds(pl.multiple_of(step * lanes, lanes), lanes)],
            vals.at[step], vals_sem.at[step],
        )

    for step in range(steps):
        load(step).start()
    beside = jnp.minimum(z, reach) + jnp.minimum(n_row - 1 - z, reach)
    pl.semaphore_wait(barrier, chips + beside)

    for q in range(halves):
        keep(q).wait()
        for cut in range(cuts):
            for d in range(1, chips):
                far(d, q, cut).start()
            near(0, q, cut).start()
    for copy in smalls[3:]:
        copy.start()
    for copy in smalls[:3]:
        copy.wait()

    slot = lax.broadcasted_iota(jnp.int32, (1, slots), 1)
    place = cols_in[...] * row_tiles + rows_in[...]
    place = jnp.where(slot < live[...], place, -1)

    @pl.loop(0, tiles_in // 128)
    def _(at):
        first = pl.multiple_of(at * 128, 128)
        index = first + lax.broadcasted_iota(jnp.int32, (128, slots), 0)
        pick[pl.ds(first, 128), :] = jnp.where(index == place, 1.0, 0.0).astype(jnp.bfloat16)

    @pl.loop(0, col_tiles)
    def _(c):
        low = pl.multiple_of(c * 2 * TILE, 2 * TILE)
        for q in range(halves):
            wide[q, pl.ds(low, TILE), part:] = jnp.zeros((TILE, part), jnp.bfloat16)
            wide[q, pl.ds(low + TILE, TILE), :part] = jnp.zeros((TILE, part), jnp.bfloat16)

    def densify(step, held, at_piece):
        def one_chunk(at, carry):
            first = pl.multiple_of(at * chunk, chunk)
            for low in range(at_piece * piece, (at_piece + 1) * piece, 256):
                sums = jnp.dot(
                    pick[pl.ds(first, chunk), :], vals[step, :, low : low + 256],
                    preferred_element_type=jnp.float32,
                ).astype(jnp.bfloat16)
                for block in range(2):
                    down = pl.ds((low // LANES + block) * row_tiles, row_tiles)
                    for c in range(chunk_cols):
                        lane = pl.multiple_of((at * chunk_cols + c) * LANES, LANES)
                        dense[held, down, pl.ds(lane, LANES)] = sums[
                            c * row_tiles : (c + 1) * row_tiles,
                            block * LANES : (block + 1) * LANES,
                        ]
            return carry

        if chunk == tiles_in:
            one_chunk(0, 0)
        else:
            lax.fori_loop(0, tiles_in // chunk, one_chunk, 0)

    def relay(q):
        for d in range(1, chips):
            for cut in range(cuts):
                far(d, q, cut).wait_recv()
                near(d, q, cut).start()

    def spread(q):
        for d in range(chips):
            for cut in range(cuts):
                near(d, q, cut).wait_recv()

        @pl.loop(0, col_tiles, unroll=4)
        def _(c):
            rows = src[q, pl.ds(pl.multiple_of(c * TILE, TILE), TILE), :]
            low = pl.multiple_of(c * 2 * TILE, 2 * TILE)
            wide[q, pl.ds(low, TILE), :part] = rows
            wide[q, pl.ds(low + TILE, TILE), part:] = rows

    def multiply(unit, held, q):
        sums = jnp.dot(dense[held], wide[q], preferred_element_type=jnp.float32)
        for block in range(blocks):
            for owner in range(n_row):
                low = block * row_tiles + owner * own
                for side in range(2):
                    to = (2 * block + side) * own
                    acc[unit, owner, to : to + own, :] = sums[
                        low : low + own, side * part : (side + 1) * part
                    ]

    def passed(u, o, to, is_up):
        land, sem = (up_in, up_sem) if is_up else (down_in, down_sem)
        return pltpu.make_async_remote_copy(
            src_ref=land.at[u, o], dst_ref=land.at[u, o],
            send_sem=send_sem.at[u, o], recv_sem=sem.at[u, o],
            device_id={"row": to}, device_id_type=MESH,
        )

    def pass_on(u, is_first, is_up, to, owner_of, begin, end):
        land = up_in if is_up else down_in

        def one(j, carry):
            o = owner_of(j)

            @pl.when(is_first)
            def _():
                land[u, o] = acc[u, o].astype(jnp.bfloat16)

            @pl.when(jnp.logical_not(is_first))
            def _():
                passed(u, o, to, is_up).wait_recv()
                land[u, o] = (acc[u, o] + land[u, o].astype(jnp.float32)).astype(jnp.bfloat16)

            passed(u, o, to, is_up).start()
            return carry

        lax.fori_loop(begin, end, one, 0)

    late_from = units // 2
    above_count = n_row - 1 - z
    below_count = z
    above_early = jnp.minimum(above_count, jnp.maximum(above_count - 1, 1))
    below_early = jnp.minimum(below_count, jnp.maximum(below_count - 1, 1))

    def pass_up(u, begin, end):
        pass_on(u, z == 0, True, z + 1, lambda j: n_row - 1 - j, begin, end)

    def pass_down(u, begin, end):
        pass_on(u, z == n_row - 1, False, z - 1, lambda j: j, begin, end)

    def chain_exchange(t):
        up = t - LAG * z

        @pl.when(jnp.logical_and(up >= 0, up < units))
        def _():
            pass_up(up, 0, jnp.where(up < late_from, above_count, above_early))

        below = t - LAG * (n_row - 1 - z)

        @pl.when(jnp.logical_and(below >= 0, below < units))
        def _():
            pass_down(below, 0, jnp.where(below < late_from, below_count, below_early))

    is_end = jnp.logical_or(z == 0, z == n_row - 1)
    is_low = z < 2
    end_of = jnp.where(is_low, 0, n_row - 1)
    middle_of = jnp.where(is_low, 1, n_row - 2)
    far_middle = n_row - 1 - middle_of
    far_end = n_row - 1 - end_of

    def sent(u, o, to, at):
        return pltpu.make_async_remote_copy(
            src_ref=down_in.at[u, o], dst_ref=up_in.at[u, at],
            send_sem=send_sem.at[u, o], recv_sem=up_sem.at[u, at],
            device_id={"row": to}, device_id_type=MESH,
        )

    def send(u, o, to, at):
        down_in[u, o] = acc[u, o].astype(jnp.bfloat16)
        sent(u, o, to, at).start()

    def first_sends(u):
        @pl.when(is_end)
        def _():
            send(u, far_end, middle_of, middle_of)
            send(u, far_middle, middle_of, far_end)

        @pl.when(jnp.logical_not(is_end))
        def _():
            send(u, end_of, end_of, z)

    def forward(u):
        @pl.when(jnp.logical_not(is_end))
        def _():
            for o, at in ((far_end, z), (far_middle, far_end)):
                sent(u, far_end, far_end, at).wait_recv()
                down_in[u, o] = (
                    acc[u, o] + up_in[u, at].astype(jnp.float32)
                ).astype(jnp.bfloat16)
                sent(u, o, o, z).start()

    def last_sends(u):
        @pl.when(is_end)
        def _():
            send(u, middle_of, middle_of, z)

    pieces = lanes // piece

    def one_step(step, carry):
        load(step).wait()
        for k in range(pieces):
            densify(step, 0, k)

        @pl.when(step == 0)
        def _():
            for q in range(halves):
                relay(q)
                spread(q)

        for q in range(halves):
            multiply(step * halves + q, 0, q)
            chain_exchange(step * halves + q)
        return carry

    def rest(t, carry):
        chain_exchange(t)
        return carry

    def late(u, carry):
        pass_up(u, above_early, above_count)
        pass_down(u, below_early, below_count)
        return carry

    if direct:
        for action in PLAN:
            what, at, k = action[0], int(action[1]), int(action[2])
            unit = at * halves + k
            if what == "d":
                if k == 0:
                    load(at).wait()
                densify(at, at, k)
            elif what == "r":
                relay(at)
            elif what == "s":
                spread(at)
            elif what == "m":
                multiply(unit, at, k)
            elif what == "x":
                first_sends(unit)
            elif what == "f":
                forward(unit)
            elif what == "l":
                last_sends(unit)
    else:
        lax.fori_loop(0, steps, one_step, 0)
        lax.fori_loop(units, units + LAG * (n_row - 1), rest, 0)
        lax.fori_loop(late_from, units, late, 0)

    for copy in smalls[3:]:
        copy.wait()

    part_rows = acc.shape[2]
    per_final = final.shape[1] // part_rows

    def direct_total(u, q, down):
        sent(u, z, z, far_middle).wait_recv()

        @pl.when(is_end)
        def _():
            sent(u, z, z, middle_of).wait_recv()
            final[q, down, :] = (
                acc[u, z] + up_in[u, middle_of].astype(jnp.float32)
            ) + up_in[u, far_middle].astype(jnp.float32)

        @pl.when(jnp.logical_not(is_end))
        def _():
            sent(u, z, z, end_of).wait_recv()
            final[q, down, :] = (
                acc[u, z] + up_in[u, far_middle].astype(jnp.float32)
            ) + up_in[u, end_of].astype(jnp.float32)

    def chain_total(u, q, down):
        @pl.when(z > 0)
        def _():
            passed(u, z, z + 1, True).wait_recv()

        @pl.when(z < n_row - 1)
        def _():
            passed(u, z, z - 1, False).wait_recv()

        @pl.when(z == 0)
        def _():
            final[q, down, :] = acc[u, z] + down_in[u, z].astype(jnp.float32)

        @pl.when(z == n_row - 1)
        def _():
            final[q, down, :] = acc[u, z] + up_in[u, z].astype(jnp.float32)

        @pl.when(jnp.logical_and(z > 0, z < n_row - 1))
        def _():
            final[q, down, :] = (
                acc[u, z] + up_in[u, z].astype(jnp.float32)
            ) + down_in[u, z].astype(jnp.float32)

    def finish(at, carry):
        for k in range(per_final):
            step = at * per_final + k
            for q in range(halves):
                u = step * halves + q
                down = slice(k * part_rows, (k + 1) * part_rows)

                (direct_total if direct else chain_total)(u, q, down)

        hidden = jnp.concatenate(
            [
                jnp.concatenate(
                    [final[q, pl.ds(r, FINAL, own), :] for r in range(own)], axis=0
                )
                for q in range(halves)
            ],
            axis=1,
        ).astype(jnp.bfloat16)
        mixed = jnp.dot(hidden, weight[...], preferred_element_type=jnp.float32) + bias[...]
        mixed = jnp.maximum(mixed, 0.0).astype(jnp.bfloat16)
        for r in range(own):
            out_ref[r, pl.ds(pl.multiple_of(at * FINAL, FINAL), FINAL), :] = mixed[
                r * FINAL : (r + 1) * FINAL
            ]
        return carry

    lax.fori_loop(0, TILE // FINAL, finish, 0)

    for q in range(halves):
        for d in range(1, chips):
            for cut in range(cuts):
                far(d, q, cut).wait_send()
        for d in range(chips):
            for cut in range(cuts):
                near(d, q, cut).wait_send()

    def drain(u, carry):
        if direct:
            for o in range(n_row):

                @pl.when(z != o)
                def _():
                    sent(u, o, o, z).wait_send()

            return carry

        def up_one(o, inner):
            passed(u, o, z + 1, True).wait_send()
            return inner

        def down_one(o, inner):
            passed(u, o, z - 1, False).wait_send()
            return inner

        lax.fori_loop(z + 1, n_row, up_one, 0)
        lax.fori_loop(0, z, down_one, 0)
        return carry

    lax.fori_loop(0, units, drain, 0)


def on_device(features, tile_values, tile_rows, tile_cols, counts, weight, bias):
    n_row, n_col = lax.axis_size("row"), lax.axis_size("col")
    piece_rows, width = features.shape[1:]
    slots, entries = tile_values.shape[2:]
    own = piece_rows // TILE
    row_tiles = n_row * own
    source_rows = n_col * piece_rows
    tiles_in = row_tiles * source_rows // TILE
    steps, held, piece = (4, 4, 512) if n_row == 4 else (16, 1, 256)
    lanes = entries // steps
    blocks = lanes // LANES
    halves = width // LANES
    cuts = 4
    part_rows = 2 * blocks * own
    slabs = (steps * halves, n_row, part_rows, LANES)
    dma = pltpu.SemaphoreType.DMA
    anywhere = pl.BlockSpec(memory_space=pl.ANY)
    out = pl.pallas_call(
        functools.partial(layer_kernel, n_row, n_col, piece),
        in_specs=[anywhere] * 7,
        out_specs=pl.BlockSpec(memory_space=pltpu.VMEM),
        out_shape=jax.ShapeDtypeStruct((own, TILE, width), jnp.bfloat16),
        scratch_shapes=[
            pltpu.VMEM((steps, slots, lanes), jnp.bfloat16),
            pltpu.VMEM((1, 1), jnp.int32),
            pltpu.VMEM((1, slots), jnp.int32),
            pltpu.VMEM((1, slots), jnp.int32),
            pltpu.VMEM((width, width), jnp.bfloat16),
            pltpu.VMEM((1, width), jnp.float32),
            pltpu.VMEM((tiles_in, slots), jnp.bfloat16),
            pltpu.VMEM((held, blocks * row_tiles, 2 * source_rows), jnp.bfloat16),
            pltpu.VMEM((halves, source_rows, LANES), jnp.bfloat16),
            pltpu.VMEM((halves, 2 * source_rows, 2 * LANES), jnp.bfloat16),
            pltpu.VMEM(slabs, jnp.float32),
            pltpu.VMEM(slabs, jnp.bfloat16),
            pltpu.VMEM(slabs, jnp.bfloat16),
            pltpu.VMEM((halves, FINAL * own, LANES), jnp.float32),
            dma((steps,)), dma((5,)), dma((halves,)),
            dma((n_col // 2, halves, cuts)), dma((n_col // 2, halves, cuts)),
            dma((n_col // 2, halves, cuts)), dma((n_col // 2, halves, cuts)),
            dma((steps * halves, n_row)), dma((steps * halves, n_row)),
            dma((steps * halves, n_row)),
        ],
        compiler_params=pltpu.CompilerParams(
            collective_id=0, has_side_effects=True, vmem_limit_bytes=62 * 1024 * 1024
        ),
    )(counts, tile_values, tile_rows, tile_cols, features, weight, bias.reshape(1, width))
    return out.reshape(1, piece_rows, width)


def solution(mesh):
    in_specs = (
        P(("groups", "row"), "col", None),
        P(("groups", "row"), "col", None, None),
        P(("groups", "row"), "col", None),
        P(("groups", "row"), "col", None),
        P(("groups", "row"), "col"),
        P(),
        P(),
    )
    out_specs = P(("groups", "col"), "row", None)
    return jax.shard_map(
        on_device, mesh=mesh, in_specs=in_specs, out_specs=out_specs, check_vma=False
    )
```

```python
import functools

import jax
import jax.numpy as jnp
from jax import lax
from jax.experimental import pallas as pl
from jax.experimental.pallas import tpu as pltpu
from jax.sharding import PartitionSpec as P

TILE = 64
LANES = 128
FINAL = 16
LAG = 2
PLAN = (
    "d00", "d01", "D10", "r00", "D11", "s00", "m00", "x00", "r10", "l00", "D20", "s10",
    "m01", "x01", "f00", "M10", "x10", "x11", "D21", "f01", "M20", "x20", "x21", "f10",
    "f11", "D30", "f20", "f21", "D31", "M30", "x30", "x31", "f30", "f31", "l10", "l01",
    "l11", "l20", "l21", "l30", "l31",
)
MESH = pl.DeviceIdType.MESH


def layer_kernel(
    n_row, n_col, piece, counts_hbm, vals_hbm, rows_hbm, cols_hbm, feat_hbm, weight_hbm, bias_hbm,
    out_ref, vals, live, rows_in, cols_in, weight, bias, pick, dense, src, wide, whole, acc, up_in, down_in,
    final, vals_sem, small_sem, own_sem, far_send, far_recv, near_send, near_recv, send_sem, up_sem,
    down_sem,
):
    steps, slots, lanes = vals.shape
    halves, source_rows, part = src.shape
    cuts = far_send.shape[2]
    tiles_in = pick.shape[0]
    piece_rows = feat_hbm.shape[1]
    col_tiles = source_rows // TILE
    row_tiles = tiles_in // col_tiles
    chunk = min(tiles_in, 1024)
    chunk_cols = chunk // row_tiles
    own = row_tiles // n_row
    blocks = lanes // LANES
    units = steps * halves
    chips = n_col // 2
    z = lax.axis_index("row")
    me = lax.axis_index("col")
    core = lax.rem(me, 2)
    sibling = me + 1 - 2 * core

    barrier = pltpu.get_barrier_semaphore()
    for d in range(1, chips):
        pl.semaphore_signal(
            barrier, inc=1, device_id={"col": lax.rem(me + 2 * d, n_col)}, device_id_type=MESH
        )
    pl.semaphore_signal(barrier, inc=1, device_id={"col": sibling}, device_id_type=MESH)

    direct = n_row == 4
    reach = 2 if direct else 1
    for d in range(1, reach + 1):

        @pl.when(z >= d)
        def _():
            pl.semaphore_signal(barrier, inc=1, device_id={"row": z - d}, device_id_type=MESH)

        @pl.when(z < n_row - d)
        def _():
            pl.semaphore_signal(barrier, inc=1, device_id={"row": z + d}, device_id_type=MESH)

    smalls = [
        pltpu.make_async_copy(rows_hbm.at[0], rows_in, small_sem.at[0]),
        pltpu.make_async_copy(cols_hbm.at[0], cols_in, small_sem.at[1]),
        pltpu.make_async_copy(counts_hbm, live, small_sem.at[2]),
        pltpu.make_async_copy(weight_hbm, weight, small_sem.at[3]),
        pltpu.make_async_copy(bias_hbm, bias, small_sem.at[4]),
    ]
    cut_rows = piece_rows // cuts

    def rows_of(index, q, cut):
        first = pl.multiple_of(index * piece_rows + cut * cut_rows, cut_rows)
        return src.at[q, pl.ds(first, cut_rows)]

    def far(d, q, cut):
        return pltpu.make_async_remote_copy(
            src_ref=rows_of(me, q, cut), dst_ref=rows_of(me, q, cut),
            send_sem=far_send.at[d, q, cut], recv_sem=far_recv.at[d, q, cut],
            device_id={"col": lax.rem(me + 2 * d, n_col)}, device_id_type=MESH,
        )

    def near(d, q, cut):
        origin = lax.rem(me + n_col - 2 * d, n_col)
        return pltpu.make_async_remote_copy(
            src_ref=rows_of(origin, q, cut), dst_ref=rows_of(origin, q, cut),
            send_sem=near_send.at[d, q, cut], recv_sem=near_recv.at[d, q, cut],
            device_id={"col": sibling}, device_id_type=MESH,
        )

    def keep(q):
        return pltpu.make_async_copy(
            feat_hbm.at[0, :, pl.ds(q * part, part)],
            src.at[q, pl.ds(pl.multiple_of(me * piece_rows, piece_rows), piece_rows)],
            own_sem.at[q],
        )

    for q in range(halves):
        keep(q).start()
    for copy in smalls[:3]:
        copy.start()

    def load(step):
        return pltpu.make_async_copy(
            vals_hbm.at[0, 0, :, pl.ds(pl.multiple_of(step * lanes, lanes), lanes)],
            vals.at[step], vals_sem.at[step],
        )

    for step in range(steps):
        load(step).start()
    beside = jnp.minimum(z, reach) + jnp.minimum(n_row - 1 - z, reach)
    pl.semaphore_wait(barrier, chips + beside)

    for q in range(halves):
        keep(q).wait()
        for cut in range(cuts):
            for d in range(1, chips):
                far(d, q, cut).start()
            near(0, q, cut).start()
    for copy in smalls[3:]:
        copy.start()
    for copy in smalls[:3]:
        copy.wait()

    slot = lax.broadcasted_iota(jnp.int32, (1, slots), 1)
    place = cols_in[...] * row_tiles + rows_in[...]
    place = jnp.where(slot < live[...], place, -1)

    @pl.loop(0, tiles_in // 128)
    def _(at):
        first = pl.multiple_of(at * 128, 128)
        index = first + lax.broadcasted_iota(jnp.int32, (128, slots), 0)
        pick[pl.ds(first, 128), :] = jnp.where(index == place, 1.0, 0.0).astype(jnp.bfloat16)

    @pl.loop(0, col_tiles)
    def _(c):
        low = pl.multiple_of(c * 2 * TILE, 2 * TILE)
        for q in range(halves):
            wide[q, pl.ds(low, TILE), part:] = jnp.zeros((TILE, part), jnp.bfloat16)
            wide[q, pl.ds(low + TILE, TILE), :part] = jnp.zeros((TILE, part), jnp.bfloat16)

    is_low = lax.broadcasted_iota(jnp.int32, (row_tiles, LANES), 1) < TILE

    def densify(step, held, at_piece, turning=False):
        def one_chunk(at, carry):
            first = pl.multiple_of(at * chunk, chunk)
            for low in range(at_piece * piece, (at_piece + 1) * piece, 256):
                sums = jnp.dot(
                    pick[pl.ds(first, chunk), :], vals[step, :, low : low + 256],
                    preferred_element_type=jnp.float32,
                )
                for block in range(2):
                    down = pl.ds((low // LANES + block) * row_tiles, row_tiles)

                    def tiles(c):
                        return sums[
                            c * row_tiles : (c + 1) * row_tiles,
                            block * LANES : (block + 1) * LANES,
                        ]

                    if turning:
                        for pair in range(chunk_cols // 2):
                            even = tiles(2 * pair)
                            odd = pltpu.roll(tiles(2 * pair + 1), TILE, 1)
                            lane = pair * LANES
                            dense[held, down, pl.ds(lane, LANES)] = jnp.where(
                                is_low, even, odd
                            ).astype(jnp.bfloat16)
                            dense[held, down, pl.ds(source_rows + lane, LANES)] = jnp.where(
                                is_low, odd, even
                            ).astype(jnp.bfloat16)
                    else:
                        for c in range(chunk_cols):
                            lane = pl.multiple_of((at * chunk_cols + c) * LANES, LANES)
                            dense[held, down, pl.ds(lane, LANES)] = tiles(c).astype(jnp.bfloat16)
            return carry

        if chunk == tiles_in:
            one_chunk(0, 0)
        else:
            lax.fori_loop(0, tiles_in // chunk, one_chunk, 0)

    def relay(q, which=None):
        for d in range(1, chips):
            for cut in range(cuts) if which is None else (which,):
                far(d, q, cut).wait_recv()
                near(d, q, cut).start()

    def spread(q):
        for d in range(chips):
            for cut in range(cuts):
                near(d, q, cut).wait_recv()

        @pl.loop(0, col_tiles, unroll=4)
        def _(c):
            rows = src[q, pl.ds(pl.multiple_of(c * TILE, TILE), TILE), :]
            low = pl.multiple_of(c * 2 * TILE, 2 * TILE)
            wide[q, pl.ds(low, TILE), :part] = rows
            wide[q, pl.ds(low + TILE, TILE), part:] = rows
            if direct:
                other = pl.multiple_of((c + 1 - 2 * lax.rem(c, 2)) * TILE, TILE)
                whole[0, pl.ds(pl.multiple_of(c * TILE, TILE), TILE), q * part : (q + 1) * part] = rows
                whole[1, pl.ds(other, TILE), q * part : (q + 1) * part] = rows

    def multiply(unit, held, q):
        sums = jnp.dot(dense[held], wide[q], preferred_element_type=jnp.float32)
        for block in range(blocks):
            for owner in range(n_row):
                low = block * row_tiles + owner * own
                for side in range(2):
                    to = (2 * block + side) * own
                    acc[unit, owner, to : to + own, :] = sums[
                        low : low + own, side * part : (side + 1) * part
                    ]

    def multiply_whole(step, held):
        for side in range(2):
            sums = jnp.dot(
                dense[held, :, side * source_rows : (side + 1) * source_rows], whole[side],
                preferred_element_type=jnp.float32,
            )
            for q in range(halves):
                for block in range(blocks):
                    for owner in range(n_row):
                        low = block * row_tiles + owner * own
                        to = (2 * block + side) * own
                        acc[step * halves + q, owner, to : to + own, :] = sums[
                            low : low + own, q * part : (q + 1) * part
                        ]

    def passed(u, o, to, is_up):
        land, sem = (up_in, up_sem) if is_up else (down_in, down_sem)
        return pltpu.make_async_remote_copy(
            src_ref=land.at[u, o], dst_ref=land.at[u, o],
            send_sem=send_sem.at[u, o], recv_sem=sem.at[u, o],
            device_id={"row": to}, device_id_type=MESH,
        )

    def pass_on(u, is_first, is_up, to, owner_of, begin, end):
        land = up_in if is_up else down_in

        def one(j, carry):
            o = owner_of(j)

            @pl.when(is_first)
            def _():
                land[u, o] = acc[u, o].astype(jnp.bfloat16)

            @pl.when(jnp.logical_not(is_first))
            def _():
                passed(u, o, to, is_up).wait_recv()
                land[u, o] = (acc[u, o] + land[u, o].astype(jnp.float32)).astype(jnp.bfloat16)

            passed(u, o, to, is_up).start()
            return carry

        lax.fori_loop(begin, end, one, 0)

    late_from = units // 2
    above_count = n_row - 1 - z
    below_count = z
    above_early = jnp.minimum(above_count, jnp.maximum(above_count - 1, 1))
    below_early = jnp.minimum(below_count, jnp.maximum(below_count - 1, 1))

    def pass_up(u, begin, end):
        pass_on(u, z == 0, True, z + 1, lambda j: n_row - 1 - j, begin, end)

    def pass_down(u, begin, end):
        pass_on(u, z == n_row - 1, False, z - 1, lambda j: j, begin, end)

    def chain_exchange(t):
        up = t - LAG * z

        @pl.when(jnp.logical_and(up >= 0, up < units))
        def _():
            pass_up(up, 0, jnp.where(up < late_from, above_count, above_early))

        below = t - LAG * (n_row - 1 - z)

        @pl.when(jnp.logical_and(below >= 0, below < units))
        def _():
            pass_down(below, 0, jnp.where(below < late_from, below_count, below_early))

    is_end = jnp.logical_or(z == 0, z == n_row - 1)
    is_below = z < 2
    end_of = jnp.where(is_below, 0, n_row - 1)
    middle_of = jnp.where(is_below, 1, n_row - 2)
    far_middle = n_row - 1 - middle_of
    far_end = n_row - 1 - end_of

    def sent(u, o, to, at):
        return pltpu.make_async_remote_copy(
            src_ref=down_in.at[u, o], dst_ref=up_in.at[u, at],
            send_sem=send_sem.at[u, o], recv_sem=up_sem.at[u, at],
            device_id={"row": to}, device_id_type=MESH,
        )

    def send(u, o, to, at):
        down_in[u, o] = acc[u, o].astype(jnp.bfloat16)
        sent(u, o, to, at).start()

    def first_sends(u):
        @pl.when(is_end)
        def _():
            send(u, far_end, middle_of, middle_of)
            send(u, far_middle, middle_of, far_end)

        @pl.when(jnp.logical_not(is_end))
        def _():
            send(u, end_of, end_of, z)

    def forward(u):
        @pl.when(jnp.logical_not(is_end))
        def _():
            for o, at in ((far_end, z), (far_middle, far_end)):
                sent(u, far_end, far_end, at).wait_recv()
                down_in[u, o] = (
                    acc[u, o] + up_in[u, at].astype(jnp.float32)
                ).astype(jnp.bfloat16)
                sent(u, o, o, z).start()

    def last_sends(u):
        @pl.when(is_end)
        def _():
            send(u, middle_of, middle_of, z)

    pieces = lanes // piece

    def one_step(step, carry):
        load(step).wait()
        for k in range(pieces):
            densify(step, 0, k)

        @pl.when(step == 0)
        def _():
            for q in range(halves):
                relay(q)
                spread(q)

        for q in range(halves):
            multiply(step * halves + q, 0, q)
            chain_exchange(step * halves + q)
        return carry

    def rest(t, carry):
        chain_exchange(t)
        return carry

    def late(u, carry):
        pass_up(u, above_early, above_count)
        pass_down(u, below_early, below_count)
        return carry

    if direct:
        for action in PLAN:
            what, at, k = action[0], int(action[1]), int(action[2])
            unit = at * halves + k
            if what == "d":
                if k == 0:
                    load(at).wait()
                densify(at, at, k)
            elif what == "D":
                if k == 0:
                    load(at).wait()
                densify(at, at, k, True)
            elif what == "M":
                multiply_whole(at, at)
            elif what == "c":
                relay(at, k)
            elif what == "r":
                relay(at)
            elif what == "s":
                spread(at)
            elif what == "m":
                multiply(unit, at, k)
            elif what == "x":
                first_sends(unit)
            elif what == "f":
                forward(unit)
            elif what == "l":
                last_sends(unit)
    else:
        lax.fori_loop(0, steps, one_step, 0)
        lax.fori_loop(units, units + LAG * (n_row - 1), rest, 0)
        lax.fori_loop(late_from, units, late, 0)

    for copy in smalls[3:]:
        copy.wait()

    part_rows = acc.shape[2]
    per_final = final.shape[1] // part_rows

    def direct_total(u, q, down):
        sent(u, z, z, far_middle).wait_recv()

        @pl.when(is_end)
        def _():
            sent(u, z, z, middle_of).wait_recv()
            final[q, down, :] = (
                acc[u, z] + up_in[u, middle_of].astype(jnp.float32)
            ) + up_in[u, far_middle].astype(jnp.float32)

        @pl.when(jnp.logical_not(is_end))
        def _():
            sent(u, z, z, end_of).wait_recv()
            final[q, down, :] = (
                acc[u, z] + up_in[u, far_middle].astype(jnp.float32)
            ) + up_in[u, end_of].astype(jnp.float32)

    def chain_total(u, q, down):
        @pl.when(z > 0)
        def _():
            passed(u, z, z + 1, True).wait_recv()

        @pl.when(z < n_row - 1)
        def _():
            passed(u, z, z - 1, False).wait_recv()

        @pl.when(z == 0)
        def _():
            final[q, down, :] = acc[u, z] + down_in[u, z].astype(jnp.float32)

        @pl.when(z == n_row - 1)
        def _():
            final[q, down, :] = acc[u, z] + up_in[u, z].astype(jnp.float32)

        @pl.when(jnp.logical_and(z > 0, z < n_row - 1))
        def _():
            final[q, down, :] = (
                acc[u, z] + up_in[u, z].astype(jnp.float32)
            ) + down_in[u, z].astype(jnp.float32)

    def finish(at, carry):
        for k in range(per_final):
            step = at * per_final + k
            for q in range(halves):
                u = step * halves + q
                down = slice(k * part_rows, (k + 1) * part_rows)

                (direct_total if direct else chain_total)(u, q, down)

        hidden = jnp.concatenate(
            [
                jnp.concatenate(
                    [final[q, pl.ds(r, FINAL, own), :] for r in range(own)], axis=0
                )
                for q in range(halves)
            ],
            axis=1,
        ).astype(jnp.bfloat16)
        mixed = jnp.dot(hidden, weight[...], preferred_element_type=jnp.float32) + bias[...]
        mixed = jnp.maximum(mixed, 0.0).astype(jnp.bfloat16)
        for r in range(own):
            out_ref[r, pl.ds(pl.multiple_of(at * FINAL, FINAL), FINAL), :] = mixed[
                r * FINAL : (r + 1) * FINAL
            ]
        return carry

    lax.fori_loop(0, TILE // FINAL, finish, 0)

    for q in range(halves):
        for d in range(1, chips):
            for cut in range(cuts):
                far(d, q, cut).wait_send()
        for d in range(chips):
            for cut in range(cuts):
                near(d, q, cut).wait_send()

    def drain(u, carry):
        if direct:
            for o in range(n_row):

                @pl.when(z != o)
                def _():
                    sent(u, o, o, z).wait_send()

            return carry

        def up_one(o, inner):
            passed(u, o, z + 1, True).wait_send()
            return inner

        def down_one(o, inner):
            passed(u, o, z - 1, False).wait_send()
            return inner

        lax.fori_loop(z + 1, n_row, up_one, 0)
        lax.fori_loop(0, z, down_one, 0)
        return carry

    lax.fori_loop(0, units, drain, 0)


def on_device(features, tile_values, tile_rows, tile_cols, counts, weight, bias):
    n_row, n_col = lax.axis_size("row"), lax.axis_size("col")
    piece_rows, width = features.shape[1:]
    slots, entries = tile_values.shape[2:]
    own = piece_rows // TILE
    row_tiles = n_row * own
    source_rows = n_col * piece_rows
    tiles_in = row_tiles * source_rows // TILE
    steps, held, piece = (4, 4, 512) if n_row == 4 else (16, 1, 256)
    lanes = entries // steps
    blocks = lanes // LANES
    halves = width // LANES
    cuts = 4
    part_rows = 2 * blocks * own
    slabs = (steps * halves, n_row, part_rows, LANES)
    dma = pltpu.SemaphoreType.DMA
    anywhere = pl.BlockSpec(memory_space=pltpu.HBM)
    out = pl.pallas_call(
        functools.partial(layer_kernel, n_row, n_col, piece),
        in_specs=[anywhere] * 7,
        out_specs=pl.BlockSpec(memory_space=pltpu.VMEM),
        out_shape=pltpu.VMEM((own, TILE, width), jnp.bfloat16),
        scratch_shapes=[
            pltpu.VMEM((steps, slots, lanes), jnp.bfloat16),
            pltpu.VMEM((1, 1), jnp.int32),
            pltpu.VMEM((1, slots), jnp.int32),
            pltpu.VMEM((1, slots), jnp.int32),
            pltpu.VMEM((width, width), jnp.bfloat16),
            pltpu.VMEM((1, width), jnp.float32),
            pltpu.VMEM((tiles_in, slots), jnp.bfloat16),
            pltpu.VMEM((held, blocks * row_tiles, 2 * source_rows), jnp.bfloat16),
            pltpu.VMEM((halves, source_rows, LANES), jnp.bfloat16),
            pltpu.VMEM((halves, 2 * source_rows, 2 * LANES), jnp.bfloat16),
            pltpu.VMEM((2, source_rows if n_row == 4 else TILE, width), jnp.bfloat16),
            pltpu.VMEM(slabs, jnp.float32),
            pltpu.VMEM(slabs, jnp.bfloat16),
            pltpu.VMEM(slabs, jnp.bfloat16),
            pltpu.VMEM((halves, FINAL * own, LANES), jnp.float32),
            dma((steps,)), dma((5,)), dma((halves,)),
            dma((n_col // 2, halves, cuts)), dma((n_col // 2, halves, cuts)),
            dma((n_col // 2, halves, cuts)), dma((n_col // 2, halves, cuts)),
            dma((steps * halves, n_row)), dma((steps * halves, n_row)),
            dma((steps * halves, n_row)),
        ],
        compiler_params=pltpu.CompilerParams(
            collective_id=0, has_side_effects=True, vmem_limit_bytes=62 * 1024 * 1024
        ),
    )(counts, tile_values, tile_rows, tile_cols, features, weight, bias.reshape(1, width))
    return out.reshape(1, piece_rows, width)


def solution(mesh):
    in_specs = (
        P(("groups", "row"), "col", None),
        P(("groups", "row"), "col", None, None),
        P(("groups", "row"), "col", None),
        P(("groups", "row"), "col", None),
        P(("groups", "row"), "col"),
        P(),
        P(),
    )
    out_specs = P(("groups", "col"), "row", None)
    return jax.shard_map(
        on_device, mesh=mesh, in_specs=in_specs, out_specs=out_specs, check_vma=False
    )
```

```python
import functools

import jax
import jax.numpy as jnp
from jax import lax
from jax.experimental import pallas as pl
from jax.experimental.pallas import tpu as pltpu
from jax.sharding import PartitionSpec as P

TILE = 64
LANES = 128
FINAL = 16
LAG = 2
PLAN = (
    "d00", "d01", "D10", "r00", "D11", "s00", "m00", "g00", "r10", "n00", "l00", "D20",
    "s10", "m01", "x01", "f00", "M10", "x10", "x11", "D21", "M20", "x20", "x21", "f01",
    "f10", "D30", "f11", "f20", "D31", "M30", "x30", "x31", "f21", "f30", "f31", "l10",
    "l01", "l11", "l20", "l21", "l30", "l31",
)
MESH = pl.DeviceIdType.MESH


def layer_kernel(
    n_row, n_col, piece, counts_hbm, vals_hbm, rows_hbm, cols_hbm, feat_hbm, weight_hbm, bias_hbm,
    out_ref, vals, live, rows_in, cols_in, weight, bias, pick, dense, src, wide, whole, acc, up_in, down_in,
    final, vals_sem, small_sem, own_sem, far_send, far_recv, near_send, near_recv, send_sem, up_sem,
    down_sem,
):
    steps, slots, lanes = vals.shape
    halves, source_rows, part = src.shape
    cuts = far_send.shape[2]
    tiles_in = pick.shape[0]
    piece_rows = feat_hbm.shape[1]
    col_tiles = source_rows // TILE
    row_tiles = tiles_in // col_tiles
    chunk = min(tiles_in, 1024)
    chunk_cols = chunk // row_tiles
    own = row_tiles // n_row
    blocks = lanes // LANES
    units = steps * halves
    chips = n_col // 2
    z = lax.axis_index("row")
    me = lax.axis_index("col")
    core = lax.rem(me, 2)
    sibling = me + 1 - 2 * core

    barrier = pltpu.get_barrier_semaphore()
    for d in range(1, chips):
        pl.semaphore_signal(
            barrier, inc=1, device_id={"col": lax.rem(me + 2 * d, n_col)}, device_id_type=MESH
        )
    pl.semaphore_signal(barrier, inc=1, device_id={"col": sibling}, device_id_type=MESH)

    direct = n_row == 4
    reach = 2 if direct else 1
    for d in range(1, reach + 1):

        @pl.when(z >= d)
        def _():
            pl.semaphore_signal(barrier, inc=1, device_id={"row": z - d}, device_id_type=MESH)

        @pl.when(z < n_row - d)
        def _():
            pl.semaphore_signal(barrier, inc=1, device_id={"row": z + d}, device_id_type=MESH)

    smalls = [
        pltpu.make_async_copy(rows_hbm.at[0], rows_in, small_sem.at[0]),
        pltpu.make_async_copy(cols_hbm.at[0], cols_in, small_sem.at[1]),
        pltpu.make_async_copy(counts_hbm, live, small_sem.at[2]),
        pltpu.make_async_copy(weight_hbm, weight, small_sem.at[3]),
        pltpu.make_async_copy(bias_hbm, bias, small_sem.at[4]),
    ]
    cut_rows = piece_rows // cuts

    def rows_of(index, q, cut):
        first = pl.multiple_of(index * piece_rows + cut * cut_rows, cut_rows)
        return src.at[q, pl.ds(first, cut_rows)]

    def far(d, q, cut):
        return pltpu.make_async_remote_copy(
            src_ref=rows_of(me, q, cut), dst_ref=rows_of(me, q, cut),
            send_sem=far_send.at[d, q, cut], recv_sem=far_recv.at[d, q, cut],
            device_id={"col": lax.rem(me + 2 * d, n_col)}, device_id_type=MESH,
        )

    def near(d, q, cut):
        origin = lax.rem(me + n_col - 2 * d, n_col)
        return pltpu.make_async_remote_copy(
            src_ref=rows_of(origin, q, cut), dst_ref=rows_of(origin, q, cut),
            send_sem=near_send.at[d, q, cut], recv_sem=near_recv.at[d, q, cut],
            device_id={"col": sibling}, device_id_type=MESH,
        )

    def keep(q):
        return pltpu.make_async_copy(
            feat_hbm.at[0, :, pl.ds(q * part, part)],
            src.at[q, pl.ds(pl.multiple_of(me * piece_rows, piece_rows), piece_rows)],
            own_sem.at[q],
        )

    for q in range(halves):
        keep(q).start()
    for copy in smalls[:3]:
        copy.start()

    def load(step):
        return pltpu.make_async_copy(
            vals_hbm.at[0, 0, :, pl.ds(pl.multiple_of(step * lanes, lanes), lanes)],
            vals.at[step], vals_sem.at[step],
        )

    for step in range(steps):
        load(step).start()
    beside = jnp.minimum(z, reach) + jnp.minimum(n_row - 1 - z, reach)
    pl.semaphore_wait(barrier, chips + beside)

    for q in range(halves):
        keep(q).wait()
        for cut in range(cuts):
            for d in range(1, chips):
                far(d, q, cut).start()
            near(0, q, cut).start()
    for copy in smalls[3:]:
        copy.start()
    for copy in smalls[:3]:
        copy.wait()

    slot = lax.broadcasted_iota(jnp.int32, (1, slots), 1)
    place = cols_in[...] * row_tiles + rows_in[...]
    place = jnp.where(slot < live[...], place, -1)

    @pl.loop(0, tiles_in // 128)
    def _(at):
        first = pl.multiple_of(at * 128, 128)
        index = first + lax.broadcasted_iota(jnp.int32, (128, slots), 0)
        pick[pl.ds(first, 128), :] = jnp.where(index == place, 1.0, 0.0).astype(jnp.bfloat16)

    @pl.loop(0, col_tiles)
    def _(c):
        low = pl.multiple_of(c * 2 * TILE, 2 * TILE)
        for q in range(halves):
            wide[q, pl.ds(low, TILE), part:] = jnp.zeros((TILE, part), jnp.bfloat16)
            wide[q, pl.ds(low + TILE, TILE), :part] = jnp.zeros((TILE, part), jnp.bfloat16)

    is_low = lax.broadcasted_iota(jnp.int32, (row_tiles, LANES), 1) < TILE

    def densify(step, held, at_piece, turning=False):
        def one_chunk(at, carry):
            first = pl.multiple_of(at * chunk, chunk)
            for low in range(at_piece * piece, (at_piece + 1) * piece, 256):
                sums = jnp.dot(
                    pick[pl.ds(first, chunk), :], vals[step, :, low : low + 256],
                    preferred_element_type=jnp.float32,
                )
                for block in range(2):
                    down = pl.ds((low // LANES + block) * row_tiles, row_tiles)

                    def tiles(c):
                        return sums[
                            c * row_tiles : (c + 1) * row_tiles,
                            block * LANES : (block + 1) * LANES,
                        ]

                    if turning:
                        for pair in range(chunk_cols // 2):
                            even = tiles(2 * pair)
                            odd = pltpu.roll(tiles(2 * pair + 1), TILE, 1)
                            lane = pair * LANES
                            dense[held, down, pl.ds(lane, LANES)] = jnp.where(
                                is_low, even, odd
                            ).astype(jnp.bfloat16)
                            dense[held, down, pl.ds(source_rows + lane, LANES)] = jnp.where(
                                is_low, odd, even
                            ).astype(jnp.bfloat16)
                    else:
                        for c in range(chunk_cols):
                            lane = pl.multiple_of((at * chunk_cols + c) * LANES, LANES)
                            dense[held, down, pl.ds(lane, LANES)] = tiles(c).astype(jnp.bfloat16)
            return carry

        if chunk == tiles_in:
            one_chunk(0, 0)
        else:
            lax.fori_loop(0, tiles_in // chunk, one_chunk, 0)

    def relay(q, which=None):
        for d in range(1, chips):
            for cut in range(cuts) if which is None else (which,):
                far(d, q, cut).wait_recv()
                near(d, q, cut).start()

    def spread(q):
        for d in range(chips):
            for cut in range(cuts):
                near(d, q, cut).wait_recv()

        @pl.loop(0, col_tiles, unroll=4)
        def _(c):
            rows = src[q, pl.ds(pl.multiple_of(c * TILE, TILE), TILE), :]
            low = pl.multiple_of(c * 2 * TILE, 2 * TILE)
            wide[q, pl.ds(low, TILE), :part] = rows
            wide[q, pl.ds(low + TILE, TILE), part:] = rows
            if direct:
                other = pl.multiple_of((c + 1 - 2 * lax.rem(c, 2)) * TILE, TILE)
                whole[0, pl.ds(pl.multiple_of(c * TILE, TILE), TILE), q * part : (q + 1) * part] = rows
                whole[1, pl.ds(other, TILE), q * part : (q + 1) * part] = rows

    def multiply(unit, held, q):
        sums = jnp.dot(dense[held], wide[q], preferred_element_type=jnp.float32)
        for block in range(blocks):
            for owner in range(n_row):
                low = block * row_tiles + owner * own
                for side in range(2):
                    to = (2 * block + side) * own
                    acc[unit, owner, to : to + own, :] = sums[
                        low : low + own, side * part : (side + 1) * part
                    ]

    def multiply_whole(step, held):
        for side in range(2):
            sums = jnp.dot(
                dense[held, :, side * source_rows : (side + 1) * source_rows], whole[side],
                preferred_element_type=jnp.float32,
            )
            for q in range(halves):
                for block in range(blocks):
                    for owner in range(n_row):
                        low = block * row_tiles + owner * own
                        to = (2 * block + side) * own
                        acc[step * halves + q, owner, to : to + own, :] = sums[
                            low : low + own, q * part : (q + 1) * part
                        ]

    def passed(u, o, to, is_up):
        land, sem = (up_in, up_sem) if is_up else (down_in, down_sem)
        return pltpu.make_async_remote_copy(
            src_ref=land.at[u, o], dst_ref=land.at[u, o],
            send_sem=send_sem.at[u, o], recv_sem=sem.at[u, o],
            device_id={"row": to}, device_id_type=MESH,
        )

    def pass_on(u, is_first, is_up, to, owner_of, begin, end):
        land = up_in if is_up else down_in

        def one(j, carry):
            o = owner_of(j)

            @pl.when(is_first)
            def _():
                land[u, o] = acc[u, o].astype(jnp.bfloat16)

            @pl.when(jnp.logical_not(is_first))
            def _():
                passed(u, o, to, is_up).wait_recv()
                land[u, o] = (acc[u, o] + land[u, o].astype(jnp.float32)).astype(jnp.bfloat16)

            passed(u, o, to, is_up).start()
            return carry

        lax.fori_loop(begin, end, one, 0)

    late_from = units // 2
    above_count = n_row - 1 - z
    below_count = z
    above_early = jnp.minimum(above_count, jnp.maximum(above_count - 1, 1))
    below_early = jnp.minimum(below_count, jnp.maximum(below_count - 1, 1))

    def pass_up(u, begin, end):
        pass_on(u, z == 0, True, z + 1, lambda j: n_row - 1 - j, begin, end)

    def pass_down(u, begin, end):
        pass_on(u, z == n_row - 1, False, z - 1, lambda j: j, begin, end)

    def chain_exchange(t):
        up = t - LAG * z

        @pl.when(jnp.logical_and(up >= 0, up < units))
        def _():
            pass_up(up, 0, jnp.where(up < late_from, above_count, above_early))

        below = t - LAG * (n_row - 1 - z)

        @pl.when(jnp.logical_and(below >= 0, below < units))
        def _():
            pass_down(below, 0, jnp.where(below < late_from, below_count, below_early))

    is_end = jnp.logical_or(z == 0, z == n_row - 1)
    is_below = z < 2
    end_of = jnp.where(is_below, 0, n_row - 1)
    middle_of = jnp.where(is_below, 1, n_row - 2)
    far_middle = n_row - 1 - middle_of
    far_end = n_row - 1 - end_of

    def sent(u, o, to, at):
        return pltpu.make_async_remote_copy(
            src_ref=down_in.at[u, o], dst_ref=up_in.at[u, at],
            send_sem=send_sem.at[u, o], recv_sem=up_sem.at[u, at],
            device_id={"row": to}, device_id_type=MESH,
        )

    def send(u, o, to, at):
        down_in[u, o] = acc[u, o].astype(jnp.bfloat16)
        sent(u, o, to, at).start()

    def farthest_sends(u):
        @pl.when(is_end)
        def _():
            send(u, far_end, middle_of, middle_of)

    def next_sends(u):
        @pl.when(is_end)
        def _():
            send(u, far_middle, middle_of, far_end)

        @pl.when(jnp.logical_not(is_end))
        def _():
            send(u, end_of, end_of, z)

    def forward(u):
        @pl.when(jnp.logical_not(is_end))
        def _():
            for o, at in ((far_end, z), (far_middle, far_end)):
                sent(u, far_end, far_end, at).wait_recv()
                down_in[u, o] = (
                    acc[u, o] + up_in[u, at].astype(jnp.float32)
                ).astype(jnp.bfloat16)
                sent(u, o, o, z).start()

    def last_sends(u):
        @pl.when(is_end)
        def _():
            send(u, middle_of, middle_of, z)

    pieces = lanes // piece

    def one_step(step, carry):
        load(step).wait()
        for k in range(pieces):
            densify(step, 0, k)

        @pl.when(step == 0)
        def _():
            for q in range(halves):
                relay(q)
                spread(q)

        for q in range(halves):
            multiply(step * halves + q, 0, q)
            chain_exchange(step * halves + q)
        return carry

    def rest(t, carry):
        chain_exchange(t)
        return carry

    def late(u, carry):
        pass_up(u, above_early, above_count)
        pass_down(u, below_early, below_count)
        return carry

    if direct:
        for action in PLAN:
            what, at, k = action[0], int(action[1]), int(action[2])
            unit = at * halves + k
            if what == "d":
                if k == 0:
                    load(at).wait()
                densify(at, at, k)
            elif what == "D":
                if k == 0:
                    load(at).wait()
                densify(at, at, k, True)
            elif what == "M":
                multiply_whole(at, at)
            elif what == "c":
                relay(at, k)
            elif what == "r":
                relay(at)
            elif what == "s":
                spread(at)
            elif what == "m":
                multiply(unit, at, k)
            elif what == "x":
                farthest_sends(unit)
                next_sends(unit)
            elif what == "g":
                farthest_sends(unit)
            elif what == "n":
                next_sends(unit)
            elif what == "f":
                forward(unit)
            elif what == "l":
                last_sends(unit)
    else:
        lax.fori_loop(0, steps, one_step, 0)
        lax.fori_loop(units, units + LAG * (n_row - 1), rest, 0)
        lax.fori_loop(late_from, units, late, 0)

    for copy in smalls[3:]:
        copy.wait()

    part_rows = acc.shape[2]
    per_final = final.shape[1] // part_rows

    def direct_total(u, q, down):
        sent(u, z, z, far_middle).wait_recv()

        @pl.when(is_end)
        def _():
            sent(u, z, z, middle_of).wait_recv()
            final[q, down, :] = (
                acc[u, z] + up_in[u, middle_of].astype(jnp.float32)
            ) + up_in[u, far_middle].astype(jnp.float32)

        @pl.when(jnp.logical_not(is_end))
        def _():
            sent(u, z, z, end_of).wait_recv()
            final[q, down, :] = (
                acc[u, z] + up_in[u, far_middle].astype(jnp.float32)
            ) + up_in[u, end_of].astype(jnp.float32)

    def chain_total(u, q, down):
        @pl.when(z > 0)
        def _():
            passed(u, z, z + 1, True).wait_recv()

        @pl.when(z < n_row - 1)
        def _():
            passed(u, z, z - 1, False).wait_recv()

        @pl.when(z == 0)
        def _():
            final[q, down, :] = acc[u, z] + down_in[u, z].astype(jnp.float32)

        @pl.when(z == n_row - 1)
        def _():
            final[q, down, :] = acc[u, z] + up_in[u, z].astype(jnp.float32)

        @pl.when(jnp.logical_and(z > 0, z < n_row - 1))
        def _():
            final[q, down, :] = (
                acc[u, z] + up_in[u, z].astype(jnp.float32)
            ) + down_in[u, z].astype(jnp.float32)

    def finish(at, carry):
        for k in range(per_final):
            step = at * per_final + k
            for q in range(halves):
                u = step * halves + q
                down = slice(k * part_rows, (k + 1) * part_rows)

                (direct_total if direct else chain_total)(u, q, down)

        hidden = jnp.concatenate(
            [
                jnp.concatenate(
                    [final[q, pl.ds(r, FINAL, own), :] for r in range(own)], axis=0
                )
                for q in range(halves)
            ],
            axis=1,
        ).astype(jnp.bfloat16)
        mixed = jnp.dot(hidden, weight[...], preferred_element_type=jnp.float32) + bias[...]
        mixed = jnp.maximum(mixed, 0.0).astype(jnp.bfloat16)
        for r in range(own):
            out_ref[r, pl.ds(pl.multiple_of(at * FINAL, FINAL), FINAL), :] = mixed[
                r * FINAL : (r + 1) * FINAL
            ]
        return carry

    lax.fori_loop(0, TILE // FINAL, finish, 0)

    for q in range(halves):
        for d in range(1, chips):
            for cut in range(cuts):
                far(d, q, cut).wait_send()
        for d in range(chips):
            for cut in range(cuts):
                near(d, q, cut).wait_send()

    def drain(u, carry):
        if direct:
            for o in range(n_row):

                @pl.when(z != o)
                def _():
                    sent(u, o, o, z).wait_send()

            return carry

        def up_one(o, inner):
            passed(u, o, z + 1, True).wait_send()
            return inner

        def down_one(o, inner):
            passed(u, o, z - 1, False).wait_send()
            return inner

        lax.fori_loop(z + 1, n_row, up_one, 0)
        lax.fori_loop(0, z, down_one, 0)
        return carry

    lax.fori_loop(0, units, drain, 0)


def on_device(features, tile_values, tile_rows, tile_cols, counts, weight, bias):
    n_row, n_col = lax.axis_size("row"), lax.axis_size("col")
    piece_rows, width = features.shape[1:]
    slots, entries = tile_values.shape[2:]
    own = piece_rows // TILE
    row_tiles = n_row * own
    source_rows = n_col * piece_rows
    tiles_in = row_tiles * source_rows // TILE
    steps, held, piece = (4, 4, 512) if n_row == 4 else (16, 1, 256)
    lanes = entries // steps
    blocks = lanes // LANES
    halves = width // LANES
    cuts = 2
    part_rows = 2 * blocks * own
    slabs = (steps * halves, n_row, part_rows, LANES)
    dma = pltpu.SemaphoreType.DMA
    anywhere = pl.BlockSpec(memory_space=pltpu.HBM)
    out = pl.pallas_call(
        functools.partial(layer_kernel, n_row, n_col, piece),
        in_specs=[anywhere] * 7,
        out_specs=pl.BlockSpec(memory_space=pltpu.VMEM),
        out_shape=pltpu.VMEM((own, TILE, width), jnp.bfloat16),
        scratch_shapes=[
            pltpu.VMEM((steps, slots, lanes), jnp.bfloat16),
            pltpu.VMEM((1, 1), jnp.int32),
            pltpu.VMEM((1, slots), jnp.int32),
            pltpu.VMEM((1, slots), jnp.int32),
            pltpu.VMEM((width, width), jnp.bfloat16),
            pltpu.VMEM((1, width), jnp.float32),
            pltpu.VMEM((tiles_in, slots), jnp.bfloat16),
            pltpu.VMEM((held, blocks * row_tiles, 2 * source_rows), jnp.bfloat16),
            pltpu.VMEM((halves, source_rows, LANES), jnp.bfloat16),
            pltpu.VMEM((halves, 2 * source_rows, 2 * LANES), jnp.bfloat16),
            pltpu.VMEM((2, source_rows if n_row == 4 else TILE, width), jnp.bfloat16),
            pltpu.VMEM(slabs, jnp.float32),
            pltpu.VMEM(slabs, jnp.bfloat16),
            pltpu.VMEM(slabs, jnp.bfloat16),
            pltpu.VMEM((halves, FINAL * own, LANES), jnp.float32),
            dma((steps,)), dma((5,)), dma((halves,)),
            dma((n_col // 2, halves, cuts)), dma((n_col // 2, halves, cuts)),
            dma((n_col // 2, halves, cuts)), dma((n_col // 2, halves, cuts)),
            dma((steps * halves, n_row)), dma((steps * halves, n_row)),
            dma((steps * halves, n_row)),
        ],
        compiler_params=pltpu.CompilerParams(
            collective_id=0, has_side_effects=True, vmem_limit_bytes=62 * 1024 * 1024
        ),
    )(counts, tile_values, tile_rows, tile_cols, features, weight, bias.reshape(1, width))
    return out.reshape(1, piece_rows, width)


def solution(mesh):
    in_specs = (
        P(("groups", "row"), "col", None),
        P(("groups", "row"), "col", None, None),
        P(("groups", "row"), "col", None),
        P(("groups", "row"), "col", None),
        P(("groups", "row"), "col"),
        P(),
        P(),
    )
    out_specs = P(("groups", "col"), "row", None)
    return jax.shard_map(
        on_device, mesh=mesh, in_specs=in_specs, out_specs=out_specs, check_vma=False
    )
```

```python
import functools

import jax
import jax.numpy as jnp
from jax import lax
from jax.experimental import pallas as pl
from jax.experimental.pallas import tpu as pltpu
from jax.sharding import PartitionSpec as P

TILE = 64
LANES = 128
FINAL = 16
LAG = 2
SPLIT = 1
PLAN = (
    "d00", "d01", "D10", "r00", "D11", "s00", "m00", "g00", "r10", "n00", "l00", "D20",
    "s10", "m01", "x01", "f00", "M10", "x10", "D21", "M20", "x20", "f01", "D30", "f10",
    "D31", "f20", "M30", "x30", "f30", "l01", "l10", "l20", "l30",
)
MESH = pl.DeviceIdType.MESH


def layer_kernel(
    n_row, n_col, piece, counts_hbm, vals_hbm, rows_hbm, cols_hbm, feat_hbm, weight_hbm, bias_hbm,
    out_ref, vals, live, rows_in, cols_in, weight, bias, pick, dense, src, wide, whole, acc, up_in, down_in,
    final, vals_sem, small_sem, own_sem, far_send, far_recv, near_send, near_recv, send_sem, up_sem,
    down_sem,
):
    steps, slots, lanes = vals.shape
    halves, source_rows, part = src.shape
    cuts = far_send.shape[2]
    tiles_in = pick.shape[0]
    piece_rows = feat_hbm.shape[1]
    col_tiles = source_rows // TILE
    row_tiles = tiles_in // col_tiles
    chunk = min(tiles_in, 1024)
    chunk_cols = chunk // row_tiles
    own = row_tiles // n_row
    blocks = lanes // LANES
    units = steps * halves
    chips = n_col // 2
    z = lax.axis_index("row")
    me = lax.axis_index("col")
    core = lax.rem(me, 2)
    sibling = me + 1 - 2 * core

    barrier = pltpu.get_barrier_semaphore()
    for d in range(1, chips):
        pl.semaphore_signal(
            barrier, inc=1, device_id={"col": lax.rem(me + 2 * d, n_col)}, device_id_type=MESH
        )
    pl.semaphore_signal(barrier, inc=1, device_id={"col": sibling}, device_id_type=MESH)

    direct = n_row == 4
    reach = 2 if direct else 1
    for d in range(1, reach + 1):

        @pl.when(z >= d)
        def _():
            pl.semaphore_signal(barrier, inc=1, device_id={"row": z - d}, device_id_type=MESH)

        @pl.when(z < n_row - d)
        def _():
            pl.semaphore_signal(barrier, inc=1, device_id={"row": z + d}, device_id_type=MESH)

    smalls = [
        pltpu.make_async_copy(rows_hbm.at[0], rows_in, small_sem.at[0]),
        pltpu.make_async_copy(cols_hbm.at[0], cols_in, small_sem.at[1]),
        pltpu.make_async_copy(counts_hbm, live, small_sem.at[2]),
        pltpu.make_async_copy(weight_hbm, weight, small_sem.at[3]),
        pltpu.make_async_copy(bias_hbm, bias, small_sem.at[4]),
    ]
    cut_rows = piece_rows // cuts

    def rows_of(index, q, cut):
        first = pl.multiple_of(index * piece_rows + cut * cut_rows, cut_rows)
        return src.at[q, pl.ds(first, cut_rows)]

    def far(d, q, cut):
        return pltpu.make_async_remote_copy(
            src_ref=rows_of(me, q, cut), dst_ref=rows_of(me, q, cut),
            send_sem=far_send.at[d, q, cut], recv_sem=far_recv.at[d, q, cut],
            device_id={"col": lax.rem(me + 2 * d, n_col)}, device_id_type=MESH,
        )

    def near(d, q, cut):
        origin = lax.rem(me + n_col - 2 * d, n_col)
        return pltpu.make_async_remote_copy(
            src_ref=rows_of(origin, q, cut), dst_ref=rows_of(origin, q, cut),
            send_sem=near_send.at[d, q, cut], recv_sem=near_recv.at[d, q, cut],
            device_id={"col": sibling}, device_id_type=MESH,
        )

    def keep(q):
        return pltpu.make_async_copy(
            feat_hbm.at[0, :, pl.ds(q * part, part)],
            src.at[q, pl.ds(pl.multiple_of(me * piece_rows, piece_rows), piece_rows)],
            own_sem.at[q],
        )

    for q in range(halves):
        keep(q).start()
    for copy in smalls[:3]:
        copy.start()

    def load(step):
        return pltpu.make_async_copy(
            vals_hbm.at[0, 0, :, pl.ds(pl.multiple_of(step * lanes, lanes), lanes)],
            vals.at[step], vals_sem.at[step],
        )

    for step in range(steps):
        load(step).start()
    beside = jnp.minimum(z, reach) + jnp.minimum(n_row - 1 - z, reach)
    pl.semaphore_wait(barrier, chips + beside)

    for q in range(halves):
        keep(q).wait()
        for cut in range(cuts):
            for d in range(1, chips):
                far(d, q, cut).start()
            near(0, q, cut).start()
    for copy in smalls[3:]:
        copy.start()
    for copy in smalls[:3]:
        copy.wait()

    slot = lax.broadcasted_iota(jnp.int32, (1, slots), 1)
    place = cols_in[...] * row_tiles + rows_in[...]
    place = jnp.where(slot < live[...], place, -1)

    @pl.loop(0, tiles_in // 128)
    def _(at):
        first = pl.multiple_of(at * 128, 128)
        index = first + lax.broadcasted_iota(jnp.int32, (128, slots), 0)
        pick[pl.ds(first, 128), :] = jnp.where(index == place, 1.0, 0.0).astype(jnp.bfloat16)

    @pl.loop(0, col_tiles)
    def _(c):
        low = pl.multiple_of(c * 2 * TILE, 2 * TILE)
        for q in range(halves):
            wide[q, pl.ds(low, TILE), part:] = jnp.zeros((TILE, part), jnp.bfloat16)
            wide[q, pl.ds(low + TILE, TILE), :part] = jnp.zeros((TILE, part), jnp.bfloat16)

    is_low = lax.broadcasted_iota(jnp.int32, (row_tiles, LANES), 1) < TILE

    def densify(step, held, at_piece, turning=False):
        def one_chunk(at, carry):
            first = pl.multiple_of(at * chunk, chunk)
            for low in range(at_piece * piece, (at_piece + 1) * piece, 256):
                sums = jnp.dot(
                    pick[pl.ds(first, chunk), :], vals[step, :, low : low + 256],
                    preferred_element_type=jnp.float32,
                )
                for block in range(2):
                    down = pl.ds((low // LANES + block) * row_tiles, row_tiles)

                    def tiles(c):
                        return sums[
                            c * row_tiles : (c + 1) * row_tiles,
                            block * LANES : (block + 1) * LANES,
                        ]

                    if turning:
                        for pair in range(chunk_cols // 2):
                            even = tiles(2 * pair)
                            odd = pltpu.roll(tiles(2 * pair + 1), TILE, 1)
                            lane = pair * LANES
                            dense[held, down, pl.ds(lane, LANES)] = jnp.where(
                                is_low, even, odd
                            ).astype(jnp.bfloat16)
                            dense[held, down, pl.ds(source_rows + lane, LANES)] = jnp.where(
                                is_low, odd, even
                            ).astype(jnp.bfloat16)
                    else:
                        for c in range(chunk_cols):
                            lane = pl.multiple_of((at * chunk_cols + c) * LANES, LANES)
                            dense[held, down, pl.ds(lane, LANES)] = tiles(c).astype(jnp.bfloat16)
            return carry

        if chunk == tiles_in:
            one_chunk(0, 0)
        else:
            lax.fori_loop(0, tiles_in // chunk, one_chunk, 0)

    def relay(q, which=None):
        for d in range(1, chips):
            for cut in range(cuts) if which is None else (which,):
                far(d, q, cut).wait_recv()
                near(d, q, cut).start()

    def spread(q):
        for d in range(chips):
            for cut in range(cuts):
                near(d, q, cut).wait_recv()

        @pl.loop(0, col_tiles, unroll=4)
        def _(c):
            rows = src[q, pl.ds(pl.multiple_of(c * TILE, TILE), TILE), :]
            low = pl.multiple_of(c * 2 * TILE, 2 * TILE)
            wide[q, pl.ds(low, TILE), :part] = rows
            wide[q, pl.ds(low + TILE, TILE), part:] = rows
            if direct:
                other = pl.multiple_of((c + 1 - 2 * lax.rem(c, 2)) * TILE, TILE)
                whole[0, pl.ds(pl.multiple_of(c * TILE, TILE), TILE), q * part : (q + 1) * part] = rows
                whole[1, pl.ds(other, TILE), q * part : (q + 1) * part] = rows

    def multiply(step, held, q):
        sums = jnp.dot(dense[held], wide[q], preferred_element_type=jnp.float32)
        for block in range(blocks):
            for owner in range(n_row):
                low = block * row_tiles + owner * own
                for side in range(2):
                    to = (2 * block + side) * own
                    acc[step, owner, q, to : to + own, :] = sums[
                        low : low + own, side * part : (side + 1) * part
                    ]

    def multiply_whole(step, held):
        for side in range(2):
            sums = jnp.dot(
                dense[held, :, side * source_rows : (side + 1) * source_rows], whole[side],
                preferred_element_type=jnp.float32,
            )
            for q in range(halves):
                for block in range(blocks):
                    for owner in range(n_row):
                        low = block * row_tiles + owner * own
                        to = (2 * block + side) * own
                        acc[step, owner, q, to : to + own, :] = sums[
                            low : low + own, q * part : (q + 1) * part
                        ]

    def passed(u, o, to, is_up):
        land, sem = (up_in, up_sem) if is_up else (down_in, down_sem)
        return pltpu.make_async_remote_copy(
            src_ref=land.at[u // halves, o, u % halves],
            dst_ref=land.at[u // halves, o, u % halves],
            send_sem=send_sem.at[u, o], recv_sem=sem.at[u, o],
            device_id={"row": to}, device_id_type=MESH,
        )

    def pass_on(u, is_first, is_up, to, owner_of, begin, end):
        land = up_in if is_up else down_in
        p, q = u // halves, u % halves

        def one(j, carry):
            o = owner_of(j)

            @pl.when(is_first)
            def _():
                land[p, o, q] = acc[p, o, q].astype(jnp.bfloat16)

            @pl.when(jnp.logical_not(is_first))
            def _():
                passed(u, o, to, is_up).wait_recv()
                land[p, o, q] = (
                    acc[p, o, q] + land[p, o, q].astype(jnp.float32)
                ).astype(jnp.bfloat16)

            passed(u, o, to, is_up).start()
            return carry

        lax.fori_loop(begin, end, one, 0)

    late_from = units // 2
    above_count = n_row - 1 - z
    below_count = z
    above_early = jnp.minimum(above_count, jnp.maximum(above_count - 1, 1))
    below_early = jnp.minimum(below_count, jnp.maximum(below_count - 1, 1))

    def pass_up(u, begin, end):
        pass_on(u, z == 0, True, z + 1, lambda j: n_row - 1 - j, begin, end)

    def pass_down(u, begin, end):
        pass_on(u, z == n_row - 1, False, z - 1, lambda j: j, begin, end)

    def chain_exchange(t):
        up = t - LAG * z

        @pl.when(jnp.logical_and(up >= 0, up < units))
        def _():
            pass_up(up, 0, jnp.where(up < late_from, above_count, above_early))

        below = t - LAG * (n_row - 1 - z)

        @pl.when(jnp.logical_and(below >= 0, below < units))
        def _():
            pass_down(below, 0, jnp.where(below < late_from, below_count, below_early))

    is_end = jnp.logical_or(z == 0, z == n_row - 1)
    is_below = z < 2
    end_of = jnp.where(is_below, 0, n_row - 1)
    middle_of = jnp.where(is_below, 1, n_row - 2)
    far_middle = n_row - 1 - middle_of
    far_end = n_row - 1 - end_of

    def place_of(unit, o):
        p, q = unit
        return (p, o) if q is None else (p, o, q)

    def sent(unit, o, to, at):
        p, q = unit
        u = p * halves + (0 if q is None else q)
        return pltpu.make_async_remote_copy(
            src_ref=down_in.at[place_of(unit, o)], dst_ref=up_in.at[place_of(unit, at)],
            send_sem=send_sem.at[u, o], recv_sem=up_sem.at[u, at],
            device_id={"row": to}, device_id_type=MESH,
        )

    def send(unit, o, to, at):
        down_in[place_of(unit, o)] = acc[place_of(unit, o)].astype(jnp.bfloat16)
        sent(unit, o, to, at).start()

    def farthest_sends(u):
        @pl.when(is_end)
        def _():
            send(u, far_end, middle_of, middle_of)

    def next_sends(u):
        @pl.when(is_end)
        def _():
            send(u, far_middle, middle_of, far_end)

        @pl.when(jnp.logical_not(is_end))
        def _():
            send(u, end_of, end_of, z)

    def forward(u):
        @pl.when(jnp.logical_not(is_end))
        def _():
            for o, at in ((far_end, z), (far_middle, far_end)):
                sent(u, far_end, far_end, at).wait_recv()
                down_in[place_of(u, o)] = (
                    acc[place_of(u, o)] + up_in[place_of(u, at)].astype(jnp.float32)
                ).astype(jnp.bfloat16)
                sent(u, o, o, z).start()

    def last_sends(u):
        @pl.when(is_end)
        def _():
            send(u, middle_of, middle_of, z)

    pieces = lanes // piece

    def one_step(step, carry):
        load(step).wait()
        for k in range(pieces):
            densify(step, 0, k)

        @pl.when(step == 0)
        def _():
            for q in range(halves):
                relay(q)
                spread(q)

        for q in range(halves):
            multiply(step, 0, q)
            chain_exchange(step * halves + q)
        return carry

    def rest(t, carry):
        chain_exchange(t)
        return carry

    def late(u, carry):
        pass_up(u, above_early, above_count)
        pass_down(u, below_early, below_count)
        return carry

    if direct:
        for action in PLAN:
            what, at, k = action[0], int(action[1]), int(action[2])
            unit = (at, k if at < SPLIT else None)
            if what == "d":
                if k == 0:
                    load(at).wait()
                densify(at, at, k)
            elif what == "D":
                if k == 0:
                    load(at).wait()
                densify(at, at, k, True)
            elif what == "M":
                multiply_whole(at, at)
            elif what == "c":
                relay(at, k)
            elif what == "r":
                relay(at)
            elif what == "s":
                spread(at)
            elif what == "m":
                multiply(at, at, k)
            elif what == "x":
                farthest_sends(unit)
                next_sends(unit)
            elif what == "g":
                farthest_sends(unit)
            elif what == "n":
                next_sends(unit)
            elif what == "f":
                forward(unit)
            elif what == "l":
                last_sends(unit)
    else:
        lax.fori_loop(0, steps, one_step, 0)
        lax.fori_loop(units, units + LAG * (n_row - 1), rest, 0)
        lax.fori_loop(late_from, units, late, 0)

    for copy in smalls[3:]:
        copy.wait()

    part_rows = acc.shape[3]
    per_final = final.shape[1] // part_rows

    def direct_total(unit, to):
        sent(unit, z, z, far_middle).wait_recv()
        far_sum = up_in[place_of(unit, far_middle)].astype(jnp.float32)

        @pl.when(is_end)
        def _():
            sent(unit, z, z, middle_of).wait_recv()
            final[to] = (
                acc[place_of(unit, z)] + up_in[place_of(unit, middle_of)].astype(jnp.float32)
            ) + far_sum

        @pl.when(jnp.logical_not(is_end))
        def _():
            sent(unit, z, z, end_of).wait_recv()
            final[to] = (
                acc[place_of(unit, z)] + far_sum
            ) + up_in[place_of(unit, end_of)].astype(jnp.float32)

    def chain_total(u, q, down):
        p = u // halves

        @pl.when(z > 0)
        def _():
            passed(u, z, z + 1, True).wait_recv()

        @pl.when(z < n_row - 1)
        def _():
            passed(u, z, z - 1, False).wait_recv()

        @pl.when(z == 0)
        def _():
            final[q, down, :] = acc[p, z, q] + down_in[p, z, q].astype(jnp.float32)

        @pl.when(z == n_row - 1)
        def _():
            final[q, down, :] = acc[p, z, q] + up_in[p, z, q].astype(jnp.float32)

        @pl.when(jnp.logical_and(z > 0, z < n_row - 1))
        def _():
            final[q, down, :] = (
                acc[p, z, q] + up_in[p, z, q].astype(jnp.float32)
            ) + down_in[p, z, q].astype(jnp.float32)

    def finish(at, carry, split=False):
        if direct and split:
            for q in range(halves):
                direct_total((at, q), q)
        elif direct:
            direct_total((at, None), slice(None))
        else:
            for k in range(per_final):
                step = at * per_final + k
                for q in range(halves):
                    down = slice(k * part_rows, (k + 1) * part_rows)
                    chain_total(step * halves + q, q, down)

        hidden = jnp.concatenate(
            [
                jnp.concatenate(
                    [final[q, pl.ds(r, FINAL, own), :] for r in range(own)], axis=0
                )
                for q in range(halves)
            ],
            axis=1,
        ).astype(jnp.bfloat16)
        mixed = jnp.dot(hidden, weight[...], preferred_element_type=jnp.float32) + bias[...]
        mixed = jnp.maximum(mixed, 0.0).astype(jnp.bfloat16)
        for r in range(own):
            out_ref[r, pl.ds(pl.multiple_of(at * FINAL, FINAL), FINAL), :] = mixed[
                r * FINAL : (r + 1) * FINAL
            ]
        return carry

    if direct:
        for at in range(SPLIT):
            finish(at, 0, True)
    lax.fori_loop(SPLIT if direct else 0, TILE // FINAL, finish, 0)

    for q in range(halves):
        for d in range(1, chips):
            for cut in range(cuts):
                far(d, q, cut).wait_send()
        for d in range(chips):
            for cut in range(cuts):
                near(d, q, cut).wait_send()

    def drain(u, carry):
        def up_one(o, inner):
            passed(u, o, z + 1, True).wait_send()
            return inner

        def down_one(o, inner):
            passed(u, o, z - 1, False).wait_send()
            return inner

        lax.fori_loop(z + 1, n_row, up_one, 0)
        lax.fori_loop(0, z, down_one, 0)
        return carry

    def drain_direct(unit):
        for o in range(n_row):

            @pl.when(z != o)
            def _():
                sent(unit, o, o, z).wait_send()

    def drain_whole(p, carry):
        drain_direct((p, None))
        return carry

    if direct:
        for p in range(SPLIT):
            for q in range(halves):
                drain_direct((p, q))
        lax.fori_loop(SPLIT, steps, drain_whole, 0)
    else:
        lax.fori_loop(0, units, drain, 0)


def on_device(features, tile_values, tile_rows, tile_cols, counts, weight, bias):
    n_row, n_col = lax.axis_size("row"), lax.axis_size("col")
    piece_rows, width = features.shape[1:]
    slots, entries = tile_values.shape[2:]
    own = piece_rows // TILE
    row_tiles = n_row * own
    source_rows = n_col * piece_rows
    tiles_in = row_tiles * source_rows // TILE
    steps, held, piece = (4, 4, 512) if n_row == 4 else (16, 1, 256)
    lanes = entries // steps
    blocks = lanes // LANES
    halves = width // LANES
    cuts = 2
    part_rows = 2 * blocks * own
    slabs = (steps, n_row, halves, part_rows, LANES)
    dma = pltpu.SemaphoreType.DMA
    anywhere = pl.BlockSpec(memory_space=pltpu.HBM)
    out = pl.pallas_call(
        functools.partial(layer_kernel, n_row, n_col, piece),
        in_specs=[anywhere] * 7,
        out_specs=pl.BlockSpec(memory_space=pltpu.VMEM),
        out_shape=pltpu.VMEM((own, TILE, width), jnp.bfloat16),
        scratch_shapes=[
            pltpu.VMEM((steps, slots, lanes), jnp.bfloat16),
            pltpu.VMEM((1, 1), jnp.int32),
            pltpu.VMEM((1, slots), jnp.int32),
            pltpu.VMEM((1, slots), jnp.int32),
            pltpu.VMEM((width, width), jnp.bfloat16),
            pltpu.VMEM((1, width), jnp.float32),
            pltpu.VMEM((tiles_in, slots), jnp.bfloat16),
            pltpu.VMEM((held, blocks * row_tiles, 2 * source_rows), jnp.bfloat16),
            pltpu.VMEM((halves, source_rows, LANES), jnp.bfloat16),
            pltpu.VMEM((halves, 2 * source_rows, 2 * LANES), jnp.bfloat16),
            pltpu.VMEM((2, source_rows if n_row == 4 else TILE, width), jnp.bfloat16),
            pltpu.VMEM(slabs, jnp.float32),
            pltpu.VMEM(slabs, jnp.bfloat16),
            pltpu.VMEM(slabs, jnp.bfloat16),
            pltpu.VMEM((halves, FINAL * own, LANES), jnp.float32),
            dma((steps,)), dma((5,)), dma((halves,)),
            dma((n_col // 2, halves, cuts)), dma((n_col // 2, halves, cuts)),
            dma((n_col // 2, halves, cuts)), dma((n_col // 2, halves, cuts)),
            dma((steps * halves, n_row)), dma((steps * halves, n_row)),
            dma((steps * halves, n_row)),
        ],
        compiler_params=pltpu.CompilerParams(
            collective_id=0, has_side_effects=True, vmem_limit_bytes=62 * 1024 * 1024
        ),
    )(counts, tile_values, tile_rows, tile_cols, features, weight, bias.reshape(1, width))
    return out.reshape(1, piece_rows, width)


def solution(mesh):
    in_specs = (
        P(("groups", "row"), "col", None),
        P(("groups", "row"), "col", None, None),
        P(("groups", "row"), "col", None),
        P(("groups", "row"), "col", None),
        P(("groups", "row"), "col"),
        P(),
        P(),
    )
    out_specs = P(("groups", "col"), "row", None)
    return jax.shard_map(
        on_device, mesh=mesh, in_specs=in_specs, out_specs=out_specs, check_vma=False
    )
```

```python
import functools

import jax
import jax.numpy as jnp
from jax import lax
from jax.experimental import pallas as pl
from jax.experimental.pallas import tpu as pltpu
from jax.sharding import PartitionSpec as P

TILE = 64
LANES = 128
FINAL = 16
LAG = 2
SPLIT = 1
PLAN = (
    "d00", "d01", "D10", "r00", "D11", "s00", "m00", "g00", "r10", "n00", "l00", "D20",
    "s10", "m01", "x01", "M10", "x10", "f00", "D21", "M20", "x20", "f01", "D30", "f10",
    "D31", "f20", "M30", "x30", "f30", "l01", "l10", "l20", "l30",
)
MESH = pl.DeviceIdType.MESH


def layer_kernel(
    n_row, n_col, piece, counts_hbm, vals_hbm, rows_hbm, cols_hbm, feat_hbm, weight_hbm, bias_hbm,
    out_ref, vals, live, rows_in, cols_in, weight, bias, pick, dense, src, wide, whole, acc, up_in, down_in,
    final, vals_sem, small_sem, own_sem, far_send, far_recv, near_send, near_recv, send_sem, up_sem,
    down_sem,
):
    steps, slots, lanes = vals.shape
    halves, source_rows, part = src.shape
    cuts = far_send.shape[2]
    tiles_in = pick.shape[0]
    piece_rows = feat_hbm.shape[1]
    col_tiles = source_rows // TILE
    row_tiles = tiles_in // col_tiles
    chunk = min(tiles_in, 1024)
    chunk_cols = chunk // row_tiles
    own = row_tiles // n_row
    blocks = lanes // LANES
    units = steps * halves
    chips = n_col // 2
    z = lax.axis_index("row")
    me = lax.axis_index("col")
    core = lax.rem(me, 2)
    sibling = me + 1 - 2 * core

    barrier = pltpu.get_barrier_semaphore()
    for d in range(1, chips):
        pl.semaphore_signal(
            barrier, inc=1, device_id={"col": lax.rem(me + 2 * d, n_col)}, device_id_type=MESH
        )
    pl.semaphore_signal(barrier, inc=1, device_id={"col": sibling}, device_id_type=MESH)

    direct = n_row == 4
    reach = 2 if direct else 1
    for d in range(1, reach + 1):

        @pl.when(z >= d)
        def _():
            pl.semaphore_signal(barrier, inc=1, device_id={"row": z - d}, device_id_type=MESH)

        @pl.when(z < n_row - d)
        def _():
            pl.semaphore_signal(barrier, inc=1, device_id={"row": z + d}, device_id_type=MESH)

    smalls = [
        pltpu.make_async_copy(rows_hbm.at[0], rows_in, small_sem.at[0]),
        pltpu.make_async_copy(cols_hbm.at[0], cols_in, small_sem.at[1]),
        pltpu.make_async_copy(counts_hbm, live, small_sem.at[2]),
        pltpu.make_async_copy(weight_hbm, weight, small_sem.at[3]),
        pltpu.make_async_copy(bias_hbm, bias, small_sem.at[4]),
    ]
    cut_rows = piece_rows // cuts

    def rows_of(index, q, cut):
        first = pl.multiple_of(index * piece_rows + cut * cut_rows, cut_rows)
        return src.at[q, pl.ds(first, cut_rows)]

    def far(d, q, cut):
        return pltpu.make_async_remote_copy(
            src_ref=rows_of(me, q, cut), dst_ref=rows_of(me, q, cut),
            send_sem=far_send.at[d, q, cut], recv_sem=far_recv.at[d, q, cut],
            device_id={"col": lax.rem(me + 2 * d, n_col)}, device_id_type=MESH,
        )

    def near(d, q, cut):
        origin = lax.rem(me + n_col - 2 * d, n_col)
        return pltpu.make_async_remote_copy(
            src_ref=rows_of(origin, q, cut), dst_ref=rows_of(origin, q, cut),
            send_sem=near_send.at[d, q, cut], recv_sem=near_recv.at[d, q, cut],
            device_id={"col": sibling}, device_id_type=MESH,
        )

    def keep(q):
        return pltpu.make_async_copy(
            feat_hbm.at[0, :, pl.ds(q * part, part)],
            src.at[q, pl.ds(pl.multiple_of(me * piece_rows, piece_rows), piece_rows)],
            own_sem.at[q],
        )

    for q in range(halves):
        keep(q).start()
    for copy in smalls[:3]:
        copy.start()

    def load(step):
        return pltpu.make_async_copy(
            vals_hbm.at[0, 0, :, pl.ds(pl.multiple_of(step * lanes, lanes), lanes)],
            vals.at[step], vals_sem.at[step],
        )

    for step in range(steps):
        load(step).start()
    beside = jnp.minimum(z, reach) + jnp.minimum(n_row - 1 - z, reach)
    pl.semaphore_wait(barrier, chips + beside)

    for q in range(halves):
        keep(q).wait()
        for cut in range(cuts):
            for d in range(1, chips):
                far(d, q, cut).start()
            near(0, q, cut).start()
    for copy in smalls[3:]:
        copy.start()
    for copy in smalls[:3]:
        copy.wait()

    slot = lax.broadcasted_iota(jnp.int32, (1, slots), 1)
    place = cols_in[...] * row_tiles + rows_in[...]
    place = jnp.where(slot < live[...], place, -1)

    @pl.loop(0, tiles_in // 128)
    def _(at):
        first = pl.multiple_of(at * 128, 128)
        index = first + lax.broadcasted_iota(jnp.int32, (128, slots), 0)
        pick[pl.ds(first, 128), :] = jnp.where(index == place, 1.0, 0.0).astype(jnp.bfloat16)

    @pl.loop(0, col_tiles)
    def _(c):
        low = pl.multiple_of(c * 2 * TILE, 2 * TILE)
        for q in range(halves):
            wide[q, pl.ds(low, TILE), part:] = jnp.zeros((TILE, part), jnp.bfloat16)
            wide[q, pl.ds(low + TILE, TILE), :part] = jnp.zeros((TILE, part), jnp.bfloat16)

    is_low = lax.broadcasted_iota(jnp.int32, (row_tiles, LANES), 1) < TILE

    def densify(step, held, at_piece, turning=False):
        def one_chunk(at, carry):
            first = pl.multiple_of(at * chunk, chunk)
            for low in range(at_piece * piece, (at_piece + 1) * piece, 256):
                sums = jnp.dot(
                    pick[pl.ds(first, chunk), :], vals[step, :, low : low + 256],
                    preferred_element_type=jnp.float32,
                )
                for block in range(2):
                    down = pl.ds((low // LANES + block) * row_tiles, row_tiles)

                    def tiles(c):
                        return sums[
                            c * row_tiles : (c + 1) * row_tiles,
                            block * LANES : (block + 1) * LANES,
                        ]

                    if turning:
                        for pair in range(chunk_cols // 2):
                            even = tiles(2 * pair)
                            odd = pltpu.roll(tiles(2 * pair + 1), TILE, 1)
                            lane = pair * LANES
                            dense[held, down, pl.ds(lane, LANES)] = jnp.where(
                                is_low, even, odd
                            ).astype(jnp.bfloat16)
                            dense[held, down, pl.ds(source_rows + lane, LANES)] = jnp.where(
                                is_low, odd, even
                            ).astype(jnp.bfloat16)
                    else:
                        for c in range(chunk_cols):
                            lane = pl.multiple_of((at * chunk_cols + c) * LANES, LANES)
                            dense[held, down, pl.ds(lane, LANES)] = tiles(c).astype(jnp.bfloat16)
            return carry

        if chunk == tiles_in:
            one_chunk(0, 0)
        else:
            lax.fori_loop(0, tiles_in // chunk, one_chunk, 0)

    def relay(q, which=None):
        for d in range(1, chips):
            for cut in range(cuts) if which is None else (which,):
                far(d, q, cut).wait_recv()
                near(d, q, cut).start()

    def spread(q):
        for d in range(chips):
            for cut in range(cuts):
                near(d, q, cut).wait_recv()

        @pl.loop(0, col_tiles, unroll=4)
        def _(c):
            rows = src[q, pl.ds(pl.multiple_of(c * TILE, TILE), TILE), :]
            low = pl.multiple_of(c * 2 * TILE, 2 * TILE)
            wide[q, pl.ds(low, TILE), :part] = rows
            wide[q, pl.ds(low + TILE, TILE), part:] = rows
            if direct:
                other = pl.multiple_of((c + 1 - 2 * lax.rem(c, 2)) * TILE, TILE)
                whole[0, pl.ds(pl.multiple_of(c * TILE, TILE), TILE), q * part : (q + 1) * part] = rows
                whole[1, pl.ds(other, TILE), q * part : (q + 1) * part] = rows

    def multiply(step, held, q):
        sums = jnp.dot(dense[held], wide[q], preferred_element_type=jnp.float32)
        for block in range(blocks):
            for owner in range(n_row):
                low = block * row_tiles + owner * own
                for side in range(2):
                    to = (2 * block + side) * own
                    acc[step, owner, q, to : to + own, :] = sums[
                        low : low + own, side * part : (side + 1) * part
                    ]

    def multiply_whole(step, held):
        for side in range(2):
            sums = jnp.dot(
                dense[held, :, side * source_rows : (side + 1) * source_rows], whole[side],
                preferred_element_type=jnp.float32,
            )
            for q in range(halves):
                for block in range(blocks):
                    for owner in range(n_row):
                        low = block * row_tiles + owner * own
                        to = (2 * block + side) * own
                        acc[step, owner, q, to : to + own, :] = sums[
                            low : low + own, q * part : (q + 1) * part
                        ]

    def passed(u, o, to, is_up):
        land, sem = (up_in, up_sem) if is_up else (down_in, down_sem)
        return pltpu.make_async_remote_copy(
            src_ref=land.at[u // halves, o, u % halves],
            dst_ref=land.at[u // halves, o, u % halves],
            send_sem=send_sem.at[u, o], recv_sem=sem.at[u, o],
            device_id={"row": to}, device_id_type=MESH,
        )

    def pass_on(u, is_first, is_up, to, owner_of, begin, end):
        land = up_in if is_up else down_in
        p, q = u // halves, u % halves

        def one(j, carry):
            o = owner_of(j)

            @pl.when(is_first)
            def _():
                land[p, o, q] = acc[p, o, q].astype(jnp.bfloat16)

            @pl.when(jnp.logical_not(is_first))
            def _():
                passed(u, o, to, is_up).wait_recv()
                land[p, o, q] = (
                    acc[p, o, q] + land[p, o, q].astype(jnp.float32)
                ).astype(jnp.bfloat16)

            passed(u, o, to, is_up).start()
            return carry

        lax.fori_loop(begin, end, one, 0)

    late_from = units // 2
    above_count = n_row - 1 - z
    below_count = z
    above_early = jnp.minimum(above_count, jnp.maximum(above_count - 1, 1))
    below_early = jnp.minimum(below_count, jnp.maximum(below_count - 1, 1))

    def pass_up(u, begin, end):
        pass_on(u, z == 0, True, z + 1, lambda j: n_row - 1 - j, begin, end)

    def pass_down(u, begin, end):
        pass_on(u, z == n_row - 1, False, z - 1, lambda j: j, begin, end)

    def chain_exchange(t):
        up = t - LAG * z

        @pl.when(jnp.logical_and(up >= 0, up < units))
        def _():
            pass_up(up, 0, jnp.where(up < late_from, above_count, above_early))

        below = t - LAG * (n_row - 1 - z)

        @pl.when(jnp.logical_and(below >= 0, below < units))
        def _():
            pass_down(below, 0, jnp.where(below < late_from, below_count, below_early))

    is_end = jnp.logical_or(z == 0, z == n_row - 1)
    is_below = z < 2
    end_of = jnp.where(is_below, 0, n_row - 1)
    middle_of = jnp.where(is_below, 1, n_row - 2)
    far_middle = n_row - 1 - middle_of
    far_end = n_row - 1 - end_of

    def place_of(unit, o):
        p, q = unit
        return (p, o) if q is None else (p, o, q)

    def sent(unit, o, to, at):
        p, q = unit
        u = p * halves + (0 if q is None else q)
        return pltpu.make_async_remote_copy(
            src_ref=down_in.at[place_of(unit, o)], dst_ref=up_in.at[place_of(unit, at)],
            send_sem=send_sem.at[u, o], recv_sem=up_sem.at[u, at],
            device_id={"row": to}, device_id_type=MESH,
        )

    def send(unit, o, to, at):
        down_in[place_of(unit, o)] = acc[place_of(unit, o)].astype(jnp.bfloat16)
        sent(unit, o, to, at).start()

    def farthest_sends(u):
        @pl.when(is_end)
        def _():
            send(u, far_end, middle_of, middle_of)

    def next_sends(u):
        @pl.when(is_end)
        def _():
            send(u, far_middle, middle_of, far_end)

        @pl.when(jnp.logical_not(is_end))
        def _():
            send(u, end_of, end_of, z)

    def forward(u):
        @pl.when(jnp.logical_not(is_end))
        def _():
            for o, at in ((far_end, z), (far_middle, far_end)):
                sent(u, far_end, far_end, at).wait_recv()
                down_in[place_of(u, o)] = (
                    acc[place_of(u, o)] + up_in[place_of(u, at)].astype(jnp.float32)
                ).astype(jnp.bfloat16)
                sent(u, o, o, z).start()

    def last_sends(u):
        @pl.when(is_end)
        def _():
            send(u, middle_of, middle_of, z)

    pieces = lanes // piece

    def one_step(step, carry):
        load(step).wait()
        for k in range(pieces):
            densify(step, 0, k)

        @pl.when(step == 0)
        def _():
            for q in range(halves):
                relay(q)
                spread(q)

        for q in range(halves):
            multiply(step, 0, q)
            chain_exchange(step * halves + q)
        return carry

    def rest(t, carry):
        chain_exchange(t)
        return carry

    def late(u, carry):
        pass_up(u, above_early, above_count)
        pass_down(u, below_early, below_count)
        return carry

    if direct:
        for action in PLAN:
            what, at, k = action[0], int(action[1]), int(action[2])
            unit = (at, k if at < SPLIT else None)
            if what == "d":
                if k == 0:
                    load(at).wait()
                densify(at, at, k)
            elif what == "D":
                if k == 0:
                    load(at).wait()
                densify(at, at, k, True)
            elif what == "M":
                multiply_whole(at, at)
            elif what == "c":
                relay(at, k)
            elif what == "r":
                relay(at)
            elif what == "s":
                spread(at)
            elif what == "m":
                multiply(at, at, k)
            elif what == "x":
                farthest_sends(unit)
                next_sends(unit)
            elif what == "g":
                farthest_sends(unit)
            elif what == "n":
                next_sends(unit)
            elif what == "f":
                forward(unit)
            elif what == "l":
                last_sends(unit)
    else:
        lax.fori_loop(0, steps, one_step, 0)
        lax.fori_loop(units, units + LAG * (n_row - 1), rest, 0)
        lax.fori_loop(late_from, units, late, 0)

    for copy in smalls[3:]:
        copy.wait()

    part_rows = acc.shape[3]
    per_final = final.shape[1] // part_rows

    def direct_total(unit, to):
        sent(unit, z, z, far_middle).wait_recv()
        far_sum = up_in[place_of(unit, far_middle)].astype(jnp.float32)

        @pl.when(is_end)
        def _():
            sent(unit, z, z, middle_of).wait_recv()
            final[to] = (
                acc[place_of(unit, z)] + up_in[place_of(unit, middle_of)].astype(jnp.float32)
            ) + far_sum

        @pl.when(jnp.logical_not(is_end))
        def _():
            sent(unit, z, z, end_of).wait_recv()
            final[to] = (
                acc[place_of(unit, z)] + far_sum
            ) + up_in[place_of(unit, end_of)].astype(jnp.float32)

    def chain_total(u, q, down):
        p = u // halves

        @pl.when(z > 0)
        def _():
            passed(u, z, z + 1, True).wait_recv()

        @pl.when(z < n_row - 1)
        def _():
            passed(u, z, z - 1, False).wait_recv()

        @pl.when(z == 0)
        def _():
            final[q, down, :] = acc[p, z, q] + down_in[p, z, q].astype(jnp.float32)

        @pl.when(z == n_row - 1)
        def _():
            final[q, down, :] = acc[p, z, q] + up_in[p, z, q].astype(jnp.float32)

        @pl.when(jnp.logical_and(z > 0, z < n_row - 1))
        def _():
            final[q, down, :] = (
                acc[p, z, q] + up_in[p, z, q].astype(jnp.float32)
            ) + down_in[p, z, q].astype(jnp.float32)

    def finish(at, carry, split=False):
        if direct and split:
            for q in range(halves):
                direct_total((at, q), q)
        elif direct:
            direct_total((at, None), slice(None))
        else:
            for k in range(per_final):
                step = at * per_final + k
                for q in range(halves):
                    down = slice(k * part_rows, (k + 1) * part_rows)
                    chain_total(step * halves + q, q, down)

        hidden = jnp.concatenate(
            [
                jnp.concatenate(
                    [final[q, pl.ds(r, FINAL, own), :] for r in range(own)], axis=0
                )
                for q in range(halves)
            ],
            axis=1,
        ).astype(jnp.bfloat16)
        mixed = jnp.dot(hidden, weight[...], preferred_element_type=jnp.float32) + bias[...]
        mixed = jnp.maximum(mixed, 0.0).astype(jnp.bfloat16)
        for r in range(own):
            out_ref[r, pl.ds(pl.multiple_of(at * FINAL, FINAL), FINAL), :] = mixed[
                r * FINAL : (r + 1) * FINAL
            ]
        return carry

    if direct:
        for at in range(SPLIT):
            finish(at, 0, True)
    lax.fori_loop(SPLIT if direct else 0, TILE // FINAL, finish, 0)

    for q in range(halves):
        for d in range(1, chips):
            for cut in range(cuts):
                far(d, q, cut).wait_send()
        for d in range(chips):
            for cut in range(cuts):
                near(d, q, cut).wait_send()

    def drain(u, carry):
        def up_one(o, inner):
            passed(u, o, z + 1, True).wait_send()
            return inner

        def down_one(o, inner):
            passed(u, o, z - 1, False).wait_send()
            return inner

        lax.fori_loop(z + 1, n_row, up_one, 0)
        lax.fori_loop(0, z, down_one, 0)
        return carry

    def drain_direct(unit):
        for o in range(n_row):

            @pl.when(z != o)
            def _():
                sent(unit, o, o, z).wait_send()

    def drain_whole(p, carry):
        drain_direct((p, None))
        return carry

    if direct:
        for p in range(SPLIT):
            for q in range(halves):
                drain_direct((p, q))
        lax.fori_loop(SPLIT, steps, drain_whole, 0)
    else:
        lax.fori_loop(0, units, drain, 0)


def on_device(features, tile_values, tile_rows, tile_cols, counts, weight, bias):
    n_row, n_col = lax.axis_size("row"), lax.axis_size("col")
    piece_rows, width = features.shape[1:]
    slots, entries = tile_values.shape[2:]
    own = piece_rows // TILE
    row_tiles = n_row * own
    source_rows = n_col * piece_rows
    tiles_in = row_tiles * source_rows // TILE
    steps, held, piece = (4, 4, 512) if n_row == 4 else (16, 1, 256)
    lanes = entries // steps
    blocks = lanes // LANES
    halves = width // LANES
    cuts = 2
    part_rows = 2 * blocks * own
    slabs = (steps, n_row, halves, part_rows, LANES)
    dma = pltpu.SemaphoreType.DMA
    anywhere = pl.BlockSpec(memory_space=pltpu.HBM)
    out = pl.pallas_call(
        functools.partial(layer_kernel, n_row, n_col, piece),
        in_specs=[anywhere] * 7,
        out_specs=pl.BlockSpec(memory_space=pltpu.VMEM),
        out_shape=pltpu.VMEM((own, TILE, width), jnp.bfloat16),
        scratch_shapes=[
            pltpu.VMEM((steps, slots, lanes), jnp.bfloat16),
            pltpu.VMEM((1, 1), jnp.int32),
            pltpu.VMEM((1, slots), jnp.int32),
            pltpu.VMEM((1, slots), jnp.int32),
            pltpu.VMEM((width, width), jnp.bfloat16),
            pltpu.VMEM((1, width), jnp.float32),
            pltpu.VMEM((tiles_in, slots), jnp.bfloat16),
            pltpu.VMEM((held, blocks * row_tiles, 2 * source_rows), jnp.bfloat16),
            pltpu.VMEM((halves, source_rows, LANES), jnp.bfloat16),
            pltpu.VMEM((halves, 2 * source_rows, 2 * LANES), jnp.bfloat16),
            pltpu.VMEM((2, source_rows if n_row == 4 else TILE, width), jnp.bfloat16),
            pltpu.VMEM(slabs, jnp.float32),
            pltpu.VMEM(slabs, jnp.bfloat16),
            pltpu.VMEM(slabs, jnp.bfloat16),
            pltpu.VMEM((halves, FINAL * own, LANES), jnp.float32),
            dma((steps,)), dma((5,)), dma((halves,)),
            dma((n_col // 2, halves, cuts)), dma((n_col // 2, halves, cuts)),
            dma((n_col // 2, halves, cuts)), dma((n_col // 2, halves, cuts)),
            dma((steps * halves, n_row)), dma((steps * halves, n_row)),
            dma((steps * halves, n_row)),
        ],
        compiler_params=pltpu.CompilerParams(
            collective_id=0, has_side_effects=True, vmem_limit_bytes=62 * 1024 * 1024
        ),
    )(counts, tile_values, tile_rows, tile_cols, features, weight, bias.reshape(1, width))
    return out.reshape(1, piece_rows, width)


def solution(mesh):
    in_specs = (
        P(("groups", "row"), "col", None),
        P(("groups", "row"), "col", None, None),
        P(("groups", "row"), "col", None),
        P(("groups", "row"), "col", None),
        P(("groups", "row"), "col"),
        P(),
        P(),
    )
    out_specs = P(("groups", "col"), "row", None)
    return jax.shard_map(
        on_device, mesh=mesh, in_specs=in_specs, out_specs=out_specs, check_vma=False
    )
```
